128 devices in a mesh: seq: 16 (over x, y), head: 8 (over z, core).
Axes of the slice: x: 4, y: 4, z: 4, core: 2. Of those that a mesh axis runs over, the one named last changes fastest.
Arguments:
- tokens: bfloat16 [128, 1024, 512], P('head', 'seq'), may hold values from -6 to 6
- lengths: int32 [128], replicated, may hold values from 64 to 1024, as said below
- norm_gain: bfloat16 [512], replicated, may hold values from 0.099609375 to 1.8984375
- value_weight: bfloat16 [512, 512], replicated, may hold values from -0.25 to 0.25
- synth_logits: bfloat16 [8, 1024, 1024], P('head', 'seq'), may hold values from -9 to 9
- out_weight: bfloat16 [512, 512], replicated, may hold values from -1 to 1
- ffn_gain: bfloat16 [512], replicated, may hold values from 0.099609375 to 1.8984375
- up_weight: bfloat16 [512, 2048], replicated, may hold values from -0.25 to 0.25
- down_weight: bfloat16 [2048, 512], replicated, may hold values from -0.125 to 0.125
- cotangent: bfloat16 [128, 1024, 512], P('head', 'seq'), may hold values from -6 to 6
Outputs:
- output: bfloat16 [128, 1024, 512], P('head', 'seq')
- input_grad: float32 [128, 1024, 512], P('head', 'seq')
- norm_gain_grad: float32 [512], replicated
- value_weight_grad: float32 [512, 512], replicated
- synth_logits_grad: float32 [8, 1024, 1024], P('head', 'seq')
- out_weight_grad: float32 [512, 512], replicated
- ffn_gain_grad: float32 [512], replicated
- up_weight_grad: float32 [512, 2048], replicated
- down_weight_grad: float32 [2048, 512], replicated
The draws below stay inside these ranges and needn't reach their ends.
Inputs may be any that keep to these rules, and one draw needn't show every extreme that they name: `lengths`: among buckets 16 * k to 16 * k + 15 one has length 1024.
All inputs are finite; a program needn't handle non-finite values.
Results may differ from the reference program's by a relative error of at most 0.017.
Values may be sent and summed in bfloat16 or wider, within the bound.
No kernel may reach another device: no remote copies, remote signals or barrier semaphores. Data moves between devices by JAX's collectives and lax.ppermute only.
A program may use at most 256 MiB of HBM per device.

```python
import jax
import jax.numpy as jnp
from jax import lax

D = 512
HEADS = 8
HEAD_DIM = 64
FF = 2048
SPAN = 1024
BKT_GRP = 16
BUCKETS = 128


def draw_lengths(key, part):
    key = jax.random.fold_in(key, 7)
    key_len, key_pick = jax.random.split(key)
    drawn_len = jax.random.randint(key_len, (BUCKETS,), SPAN // 16, SPAN + 1)
    chosen = jax.random.randint(key_pick, (BUCKETS // BKT_GRP, 1), 0, BKT_GRP)
    slot_ids = jnp.arange(BKT_GRP, dtype=jnp.int32)[None, :]
    is_full = (slot_ids == chosen).reshape(BUCKETS)
    return jnp.where(is_full, SPAN, drawn_len).astype(jnp.int32)


def levels(own_key, shape, shards, low, high):
    level, own = 1.0, jax.random.fold_in(own_key, 6)
    for position, parts in shards:
        draws = jnp.exp(jax.random.uniform(jax.random.fold_in(own, position), (parts,), jnp.float32, low / len(shards), high / len(shards)))
        level = level * jnp.repeat(draws, shape[position] // parts).reshape([-1 if axis == position else 1 for axis in range(len(shape))])
    return level


def centred(key, shape, spread, limit, pieces=(), held_as=jnp.bfloat16):
    drawn = jax.random.normal(key, shape, jnp.float32) * spread
    if len(pieces) > 0:
        drawn = levels(key, shape, pieces, -0.22, 0.18) * drawn
    return jnp.clip(drawn, min=-limit, max=limit).astype(held_as)


def setup_inputs(seed: int = 0) -> dict:
    splits = jax.random.split(jax.random.key(seed), 11)
    return {
        "tokens": centred(splits[0], (BUCKETS, SPAN, D), 1.0, 6.0, ((0, 8), (1, 16))),
        "lengths": draw_lengths(jax.random.fold_in(splits[10], 71), 0),
        "norm_gain": jnp.clip(1.0 + 0.18 * jax.random.normal(splits[2], (D,), jnp.float32), 0.099609375, 1.8984375).astype(jnp.bfloat16),
        "value_weight": centred(splits[3], (D, D), D ** -0.5, 0.25),
        "synth_logits": centred(splits[4], (HEADS, SPAN, SPAN), 1.5, 9.0, ((0, 8), (1, 16))),
        "out_weight": centred(splits[5], (D, D), (D // 16) ** -0.5, 1.0),
        "ffn_gain": jnp.clip(1.0 + 0.18 * jax.random.normal(splits[6], (D,), jnp.float32), 0.099609375, 1.8984375).astype(jnp.bfloat16),
        "up_weight": centred(splits[7], (D, FF), D ** -0.5, 0.25),
        "down_weight": centred(splits[8], (FF, D), FF ** -0.5, 0.125),
        "cotangent": centred(splits[9], (BUCKETS, SPAN, D), 1.0, 6.0, ((0, 8), (1, 16))),
    }


epsilon = 1e-06
highest = lax.Precision.HIGHEST

@jax.custom_vjp
def low(v):
    return lax.optimization_barrier(v.astype(jnp.bfloat16)).astype(jnp.float32)

@jax.custom_vjp
def low_back(v):
    return v

def low_keep(v):
    return (low(v), None)

def low_pass(kept, grad):
    return (grad,)

def back_keep(v):
    return (v, None)

def back_low(kept, grad):
    return (low(grad),)
low.defvjp(low_keep, low_pass)
low_back.defvjp(back_keep, back_low)

def matmul(left, right):
    return jnp.dot(left, right, precision=highest)

def rms_scaled(values):
    return values * lax.rsqrt(lax.optimization_barrier(jnp.mean(values * values, axis=-1, keepdims=True)) + epsilon)

def block_layer(tokens, norm_gain, value_weight, synth_logits, out_weight, ffn_gain, up_weight, down_weight, length):
    keep_mask = (jnp.arange(SPAN, dtype=jnp.int32) < length).astype(tokens.dtype)
    hidden_one = low(rms_scaled(tokens) * norm_gain)
    values = low_back(low(matmul(hidden_one, value_weight)))
    per_head = values.reshape(SPAN, HEADS, HEAD_DIM)
    row_top = lax.optimization_barrier(jnp.max(synth_logits, axis=-1, keepdims=True))
    exponent = jnp.exp(synth_logits - row_top) * keep_mask
    weights = low(exponent / lax.optimization_barrier(jnp.sum(exponent, axis=-1, keepdims=True)))
    mixed_rows = jnp.einsum('hij,jhd->ihd', weights, per_head, precision=highest).reshape(SPAN, D)
    mixed_rows = low_back(low(mixed_rows * keep_mask[:, None]))
    residual = tokens + low_back(matmul(mixed_rows, out_weight))
    hidden_two = low(rms_scaled(residual) * ffn_gain)
    pre_act = low_back(matmul(hidden_two, up_weight))
    active = low(jax.nn.gelu(pre_act, approximate=False))
    return (residual + low_back(matmul(active, down_weight))) * keep_mask[:, None]

def reference(tokens, lengths, norm_gain, value_weight, synth_logits, out_weight, ffn_gain, up_weight, down_weight, cotangent):
    weights_f = tuple((array.astype(jnp.float32) for array in (norm_gain, value_weight, synth_logits, out_weight, ffn_gain, up_weight, down_weight)))

    def bucket_step(carried, entry):
        bucket_tok, bucket_cot, bucket_len = entry

        def forward(*arrays):
            return block_layer(*arrays, bucket_len)
        result, pullback = jax.vjp(forward, bucket_tok.astype(jnp.float32), *weights_f)
        gradients = pullback(bucket_cot.astype(jnp.float32))
        carried = tuple((prior + extra for prior, extra in zip(carried, gradients[1:])))
        return (carried, (result.astype(jnp.bfloat16), gradients[0]))
    start_sums = tuple((jnp.zeros(array.shape, jnp.float32) for array in weights_f))
    summed, (output, input_grad) = lax.scan(bucket_step, start_sums, (tokens, cotangent, lengths))
    return (output, input_grad, summed[0], summed[1], summed[2], summed[3], summed[4], summed[5], summed[6])
```

```python
import functools
import math

import jax
import jax.numpy as jnp
from jax import lax
from jax.experimental import pallas as pl
from jax.experimental.pallas import tpu as pltpu
from jax.sharding import PartitionSpec as P

EPS = 1e-06
ROOT_HALF = 1.0 / math.sqrt(2.0)
DENSITY = 1.0 / math.sqrt(2.0 * math.pi)
LANES = 128
CHUNK = 32
PER = LANES // CHUNK
BOTH = ("seq", "head")
bf16 = jnp.bfloat16
f32 = jnp.float32


def nt(left, right):
    return lax.dot_general(left, right, (((1,), (1,)), ((), ())), preferred_element_type=f32)


def tn(left, right):
    return lax.dot_general(left, right, (((0,), (0,)), ((), ())), preferred_element_type=f32)


def nn(left, right):
    return jnp.dot(left, right, preferred_element_type=f32)


def lane_groups(rows):
    return lax.broadcasted_iota(jnp.int32, (rows, LANES), 1) // CHUNK


def pick(groups, parts):
    out = parts[PER - 1]
    for l in range(PER - 2, -1, -1):
        out = jnp.where(groups == l, parts[l], out)
    return out


def spread(value, store):
    rows = value.shape[0] // PER
    groups = lane_groups(rows)
    for q in range(value.shape[1] // LANES):
        turned = []
        for r in range(PER):
            piece = value[r * rows : (r + 1) * rows, q * LANES : (q + 1) * LANES]
            turned.append(pltpu.roll(piece, CHUNK * r, 1) if r else piece)
        for k in range(PER):
            store(q * PER + k, pick(groups, [turned[(l - k) % PER] for l in range(PER)]))


def collect(ref, group):
    chunks, rows, _ = ref.shape
    lanes = slice(group * LANES, (group + 1) * LANES)
    groups = lane_groups(rows)
    columns = []
    for q in range(chunks // PER):
        loaded = [ref[q * PER + k, :, lanes].astype(f32) for k in range(PER)]
        parts = []
        for r in range(PER):
            mixed = pick(groups, [loaded[(l - r) % PER] for l in range(PER)])
            parts.append(pltpu.roll(mixed, LANES - CHUNK * r, 1) if r else mixed)
        columns.append(jnp.concatenate(parts, axis=0))
    return jnp.concatenate(columns, axis=1)


def places():
    seq = lax.axis_index("seq")
    head = lax.axis_index("head")
    return seq // 4, seq % 4, head // 2, head % 2


def row_keep(lens_ref, buckets, rows):
    first = lax.axis_index("head") * (lens_ref.shape[0] // lax.axis_size("head"))
    start = lax.axis_index("seq") * rows
    spot = start + lax.broadcasted_iota(jnp.int32, (rows, 1), 0)
    parts = []
    for r in range(buckets):
        length = lens_ref[first + pl.program_id(0) * buckets + r]
        parts.append((spot < length).astype(f32))
    return jnp.concatenate(parts, axis=0)


def gain_row(gain_ref):
    return gain_ref[...].astype(f32).reshape(1, gain_ref.shape[0])


def rms(values):
    scale = lax.rsqrt(jnp.mean(values * values, axis=-1, keepdims=True) + EPS)
    return values * scale, scale


def values_kernel(lens_ref, tok_ref, gain_ref, vw_ref, out_ref):
    per, rows, width = tok_ref.shape
    tok = tok_ref[...].reshape(per * rows, width).astype(f32)
    normed, _ = rms(tok)
    hidden = (normed * gain_row(gain_ref)).astype(bf16)
    val = nn(hidden, vw_ref[...]) * row_keep(lens_ref, per, rows)

    def store(chunk, block):
        out_ref[chunk] = block.astype(bf16)

    spread(val, store)


def lane_lengths(lens_ref, lanes):
    _, y, _, _ = places()
    group = lanes // CHUNK
    first = lax.axis_index("head") * group
    lane = lax.broadcasted_iota(jnp.int32, (1, lanes), 1) // CHUNK
    lens = jnp.zeros((1, lanes), jnp.int32)
    for n in range(group):
        m, l = divmod(n, PER)
        lens = jnp.where(lane == n, lens_ref[first + m * PER + (l - y + PER) % PER], lens)
    return lens


def mix_kernel(lens_ref, *refs):
    count = len(refs) - 12
    pieces = refs[:count]
    held_ref, exp_out, inv_out, mix_out = refs[count : count + 4]
    landed, held, keep, expo, inverse, mixed, sems, out_sems = refs[count + 4 :]
    span, lanes = held.shape
    _, y, z, c = places()
    half = pieces[0].shape[0] // 2
    copies = []
    for n, piece in enumerate(pieces):
        for k in range(2):
            spot = pl.multiple_of((y + k) % 2 * half, half)
            copies.append(
                pltpu.make_async_copy(
                    piece.at[pl.ds(k * half, half), :],
                    landed.at[n, pl.ds(spot, half), :],
                    sems.at[n, k],
                )
            )
    held_copy = pltpu.make_async_copy(held_ref, held, sems.at[count, 0])
    copies[0].start()
    copies[1].start()
    held_copy.start()
    for copy in copies[2:]:
        copy.start()
    lens = lane_lengths(lens_ref, lanes)
    place = lax.broadcasted_iota(jnp.int32, (span, lanes), 0)
    keep[...] = (place < lens).astype(f32).astype(bf16)
    out_copies = []
    for n in range(count):
        copies[2 * n].wait()
        copies[2 * n + 1].wait()
        core = c if n < 4 else 1 - c
        start = pl.multiple_of((((z - n % 4 + 4) % 4) * 4 + core * 2) * half, 2 * half)
        logits = landed[n].astype(f32)
        part = jnp.exp(logits - jnp.max(logits, axis=-1, keepdims=True)).astype(bf16)
        expo[n] = part
        here = start + lax.broadcasted_iota(jnp.int32, (2 * half, lanes), 0)
        inverted = jnp.where(here < lens, 1.0 / nn(part, keep[...]), 0.0)
        inverse[n] = inverted
        if n == 0:
            held_copy.wait()
        mixed[n] = (nn(part, held[...]) * inverted).astype(bf16)
        for k, (source, target) in enumerate(
            ((mixed, mix_out), (expo, exp_out), (inverse, inv_out))
        ):
            copy = pltpu.make_async_copy(
                source.at[n], target.at[pl.ds(start, 2 * half), :], out_sems.at[n, k]
            )
            copy.start()
            out_copies.append(copy)
    for copy in out_copies:
        copy.wait()


def unmix_kernel(exp_ref, gm_ref, inv_ref, mixed_ref, out_ref, g_ref, r_ref, acc_ref):
    scaled = gm_ref[...].astype(f32) * inv_ref[...]
    low = scaled.astype(bf16)
    g_ref[...] = low
    r_ref[...] = (scaled * mixed_ref[...].astype(f32)).astype(bf16)
    part = tn(exp_ref[...], low)
    step = pl.program_id(0)

    @pl.when(step == 0)
    def _():
        acc_ref[...] = part

    @pl.when(step > 0)
    def _():
        acc_ref[...] += part

    @pl.when(step == pl.num_programs(0) - 1)
    def _():
        out_ref[...] = acc_ref[...].astype(bf16)


def scores_kernel(lens_ref, g_ref, r_ref, val_ref, out_ref, keep_ref):
    span, lanes = val_ref.shape

    @pl.when(pl.program_id(0) == 0)
    def _():
        place = lax.broadcasted_iota(jnp.int32, (span, lanes), 0)
        keep_ref[...] = (place < lane_lengths(lens_ref, lanes)).astype(f32).astype(bf16)

    out = nt(g_ref[...], val_ref[...]) - nt(r_ref[...], keep_ref[...])
    out_ref[...] = out.astype(bf16)


def ffn_kernel(
    lens_ref,
    tok_ref,
    cot_ref,
    mix_ref,
    ow_ref,
    gain_ref,
    up_ref,
    down_ref,
    out_ref,
    gr_ref,
    gm_ref,
    grads_ref,
    down_acc,
    up_acc,
    ow_acc,
):
    per, rows, width = tok_ref.shape
    n = per * rows
    ff = up_ref.shape[1]
    step = up_acc.shape[2]

    @pl.when(pl.program_id(0) == 0)
    def _():
        down_acc[...] = jnp.zeros_like(down_acc)
        up_acc[...] = jnp.zeros_like(up_acc)
        ow_acc[...] = jnp.zeros_like(ow_acc)

    keep = row_keep(lens_ref, per, rows)
    tok = tok_ref[...].reshape(n, width).astype(f32)
    grad_low = (cot_ref[...].reshape(n, width).astype(f32) * keep).astype(bf16)
    mixed = jnp.concatenate(
        [collect(mix_ref, g) for g in range(per // PER)], axis=0
    ).astype(bf16)
    resid = tok + nn(mixed, ow_ref[...])
    normed, scale = rms(resid)
    gain = gain_row(gain_ref)
    hidden = (normed * gain).astype(bf16)
    ffn = jnp.zeros((n, width), f32)
    grad_hidden = jnp.zeros((n, width), f32)
    for q in range(ff // step):
        cut = slice(q * step, (q + 1) * step)
        up = up_ref[:, cut]
        down = down_ref[cut, :]
        pre = nn(hidden, up)
        cdf = 0.5 * (1.0 + lax.erf(pre * ROOT_HALF))
        slope = cdf + pre * jnp.exp(-0.5 * pre * pre) * DENSITY
        act = (pre * cdf).astype(bf16)
        ffn = ffn + nn(act, down)
        grad_pre = (nt(grad_low, down) * slope).astype(bf16)
        grad_hidden = grad_hidden + nt(grad_pre, up)
        down_acc[cut, :] += tn(act, grad_low)
        up_acc[q] += tn(hidden, grad_pre)
    out_ref[...] = ((resid + ffn) * keep).astype(bf16).reshape(per, rows, width)
    weighted = grad_hidden * gain
    back = scale * (weighted - normed * jnp.mean(weighted * normed, axis=-1, keepdims=True))
    grad_resid = grad_low.astype(f32) + back
    gr_ref[...] = grad_resid
    grad_att = grad_resid.astype(bf16)
    ow_acc[...] += tn(mixed, grad_att)
    grad_mixed = nt(grad_att, ow_ref[...]) * keep
    size = PER * rows
    for g in range(per // PER):

        def store(chunk, block, g=g):
            gm_ref[chunk, :, g * LANES : (g + 1) * LANES] = block.astype(bf16)

        spread(grad_mixed[g * size : (g + 1) * size], store)

    @pl.when(pl.program_id(0) == pl.num_programs(0) - 1)
    def _():
        half = width // 2
        for k in range(2):
            lanes = slice(k * half, (k + 1) * half)
            grads_ref[k * ff : (k + 1) * ff, :] = down_acc[:, lanes].astype(bf16)
            for q in range(ff // step):
                first = 2 * ff + (2 * q + k) * width
                grads_ref[first : first + width, :] = up_acc[q][:, lanes].astype(bf16)
            first = 4 * ff + k * width
            grads_ref[first : first + width, :] = ow_acc[:, lanes].astype(bf16)


def value_grad_kernel(lens_ref, tok_ref, vg_ref, gain_ref, vgrad_ref, part_ref, acc_ref):
    per, rows, width = tok_ref.shape
    tok = tok_ref[...].reshape(per * rows, width).astype(f32)
    normed, _ = rms(tok)
    hidden = (normed * gain_row(gain_ref)).astype(bf16)
    vgrad = (collect(vg_ref, 0) * row_keep(lens_ref, per, rows)).astype(bf16)
    vgrad_ref[...] = vgrad

    @pl.when(pl.program_id(0) == 0)
    def _():
        acc_ref[...] = jnp.zeros_like(acc_ref)

    acc_ref[...] += tn(hidden, vgrad)

    @pl.when(pl.program_id(0) == pl.num_programs(0) - 1)
    def _():
        _, tall, wide = part_ref.shape
        for i in range(width // tall):
            for j in range(width // wide):
                part_ref[i * (width // wide) + j] = acc_ref[
                    i * tall : (i + 1) * tall, j * wide : (j + 1) * wide
                ].astype(bf16)


def input_grad_kernel(tok_ref, vgrad_ref, gr_ref, gain_ref, vw_ref, out_ref):
    per, rows, width = tok_ref.shape
    tok = tok_ref[...].reshape(per * rows, width).astype(f32)
    normed, scale = rms(tok)
    weighted = nt(vgrad_ref[...], vw_ref[...]) * gain_row(gain_ref)
    back = scale * (weighted - normed * jnp.mean(weighted * normed, axis=-1, keepdims=True))
    out_ref[...] = (gr_ref[...] + back).reshape(per, rows, width)


def sum_spread_kernel(in_ref, out_ref):
    total = jnp.sum(in_ref[...].astype(f32), axis=0)
    out_ref[...] = jnp.broadcast_to(total[None], out_ref.shape).astype(bf16)


def row_total(product):
    folded = sum(
        product[:, n * LANES : (n + 1) * LANES] for n in range(product.shape[1] // LANES)
    )
    return jnp.sum(folded.T, axis=0, keepdims=True)


def finish_ffn_kernel(
    down_one,
    down_two,
    up_in,
    ow_one,
    ow_two,
    up_ref,
    gain_ref,
    down_out,
    up_out,
    ow_out,
    gain_out,
    acc_ref,
):
    q = pl.program_id(0)
    half = down_one.shape[1]
    width = up_out.shape[0]
    down_out[:, :half] = down_one[...].astype(f32)
    down_out[:, half:] = down_two[...].astype(f32)
    up_out[:, :half] = up_in[:width, :].astype(f32)
    up_out[:, half:] = up_in[width:, :].astype(f32)
    product = up_ref[...].astype(f32) * up_out[...]

    @pl.when(q == 0)
    def _():
        acc_ref[...] = product
        ow_out[:, :half] = ow_one[...].astype(f32)
        ow_out[:, half:] = ow_two[...].astype(f32)

    @pl.when(q > 0)
    def _():
        acc_ref[...] += product

    @pl.when(q == pl.num_programs(0) - 1)
    def _():
        gain_out[...] = row_total(acc_ref[...]) / gain_row(gain_ref)


def finish_value_kernel(in_ref, vw_ref, gain_ref, out_ref, gain_out):
    count, tall, wide = in_ref.shape
    across = out_ref.shape[1] // wide
    for n in range(count):
        i, j = divmod(n, across)
        out_ref[i * tall : (i + 1) * tall, j * wide : (j + 1) * wide] = in_ref[n].astype(f32)
    gain_out[...] = row_total(vw_ref[...].astype(f32) * out_ref[...]) / gain_row(gain_ref)


def params():
    return pltpu.CompilerParams(vmem_limit_bytes=58 * 1024 * 1024)


def cost(flops, size):
    return pl.CostEstimate(flops=int(flops), bytes_accessed=int(size), transcendentals=0)


def whole(*shape):
    return pl.BlockSpec(shape, lambda *_: (0,) * len(shape))


def once(*shape):
    return pl.BlockSpec(shape, lambda *_: (0,) * len(shape), pipeline_mode=pl.Buffered(1))


def shaped(dtype, *shape):
    return pltpu.HBM(shape, dtype)


def stay(*arrays):
    return [pltpu.with_memory_space_constraint(array, pltpu.HBM) for array in arrays]


def flat(x, y, z, c):
    return ((x % 4) * 4 + y % 4) * 8 + (z % 4) * 2 + c % 2


def devices():
    for i in range(128):
        s, h = divmod(i, 8)
        yield i, s // 4, s % 4, h // 2, h % 2


def shift(array, x=0, y=0, z=0, c=0):
    pairs = [(i, flat(a + x, b + y, d + z, e + c)) for i, a, b, d, e in devices()]
    return lax.ppermute(array, BOTH, pairs)


def flip(array, y=0, c=0):
    pairs = [(i, flat(a, b ^ y, d, e ^ c)) for i, a, b, d, e in devices()]
    return lax.ppermute(array, BOTH, pairs)


def to_plane(array, odd=0, back=False):
    pairs = [(i, flat(d, 2 * e + ((b & 1) ^ odd), a, b >> 1)) for i, a, b, d, e in devices()]
    if back:
        pairs = [(j, i) for i, j in pairs]
    return lax.ppermute(array, BOTH, pairs)


def swap_seq(array):
    return lax.all_to_all(array, "seq", 0, 0, tiled=True)


def swap_all(array):
    return lax.all_to_all(array, BOTH, 0, 0, tiled=True)


def after(array, *others):
    return lax.optimization_barrier((array,) + others)[0]


def at(array, index):
    return lax.dynamic_index_in_dim(array, index, 0, keepdims=False)


def shards(
    tokens,
    lengths,
    norm_gain,
    value_weight,
    synth_logits,
    out_weight,
    ffn_gain,
    up_weight,
    down_weight,
    cotangent,
):
    group, rows, width = tokens.shape
    span = synth_logits.shape[2]
    ff = up_weight.shape[1]
    blocks = span // rows
    total_rows = group * rows
    steps = group // PER
    tile = PER * rows
    _, y, z, c = places()

    def tok_spec(n):
        return pl.BlockSpec((n, rows, width), lambda m, *_: (m, 0, 0))

    def move_spec(n):
        return pl.BlockSpec((blocks, rows, n // PER * LANES), lambda m, *_: (0, 0, m))

    def row_spec(n, columns):
        return pl.BlockSpec((n, columns), lambda m, *_: (m, 0))

    def call(kernel, grid, ins, outs, shapes, flops, size, scratch=(), prefetch=0):
        return pl.pallas_call(
            kernel,
            grid_spec=pltpu.PrefetchScalarGridSpec(
                num_scalar_prefetch=prefetch,
                grid=grid,
                in_specs=ins,
                out_specs=outs,
                scratch_shapes=scratch,
            ),
            out_shape=shapes,
            compiler_params=params(),
            cost_estimate=cost(flops, size),
        )

    with jax.named_scope("logits"):
        block = synth_logits.reshape(rows, span)
        halves = [to_plane(block), to_plane(block, odd=1)]

    with jax.named_scope("values"):
        sent_values = call(
            values_kernel,
            (steps,),
            [tok_spec(PER), whole(width), whole(width, width)],
            move_spec(PER),
            shaped(bf16, blocks, rows, width),
            2 * total_rows * width * width,
            3e6,
            prefetch=1,
        )(lengths, *stay(tokens, norm_gain, value_weight))
        halves = lax.optimization_barrier((*halves, sent_values))
        sent_values = halves[2]
        held = swap_seq(sent_values).reshape(span, width)

    with jax.named_scope("logits"):
        pair = jnp.concatenate(halves[:2])
        pieces = [pair] + [shift(pair, z=step) for step in (1, 2, 3)]
        pieces = pieces + [flip(piece, c=1) for piece in pieces]

    quarter = span // 4
    with jax.named_scope("mix"):
        anywhere = pl.BlockSpec(memory_space=pl.ANY)
        expo, inverse, mixed_held = call(
            mix_kernel,
            (1,),
            [anywhere] * 9,
            [anywhere] * 3,
            [shaped(bf16, span, span), shaped(f32, span, width), shaped(bf16, span, width)],
            4 * span * span * width,
            8e6,
            scratch=[
                pltpu.VMEM((8, 2 * rows, span), bf16),
                pltpu.VMEM((span, width), bf16),
                pltpu.VMEM((span, width), bf16),
                pltpu.VMEM((8, 2 * rows, span), bf16),
                pltpu.VMEM((8, 2 * rows, width), f32),
                pltpu.VMEM((8, 2 * rows, width), bf16),
                pltpu.SemaphoreType.DMA((9, 2)),
                pltpu.SemaphoreType.DMA((8, 3)),
            ],
            prefetch=1,
        )(lengths, *stay(*pieces, held))
        got_mixed = swap_seq(mixed_held.reshape(blocks, rows, width))

    grad_rows = 4 * ff + 2 * width
    with jax.named_scope("ffn"):
        output, grad_resid, sent_grad, ffn_part = call(
            ffn_kernel,
            (steps // 2,),
            [
                tok_spec(2 * PER),
                tok_spec(2 * PER),
                move_spec(2 * PER),
                once(width, width),
                once(width),
                once(width, ff),
                once(ff, width),
            ],
            [
                tok_spec(2 * PER),
                row_spec(2 * tile, width),
                move_spec(2 * PER),
                once(grad_rows, width // 2),
            ],
            [
                shaped(bf16, group, rows, width),
                shaped(f32, total_rows, width),
                shaped(bf16, blocks, rows, width),
                shaped(bf16, grad_rows, width // 2),
            ],
            2 * total_rows * width * (6 * ff + 3 * width),
            2e7,
            scratch=[
                pltpu.VMEM((ff, width), f32),
                pltpu.VMEM((ff // width, width, width), f32),
                pltpu.VMEM((width, width), f32),
            ],
            prefetch=1,
        )(
            lengths,
            *stay(tokens, cotangent, got_mixed, out_weight, ffn_gain, up_weight, down_weight),
        )
        got_grad = swap_seq(sent_grad).reshape(span, width)

    with jax.named_scope("ffn_sum"):
        ffn_sum = lax.psum_scatter(ffn_part, "head", scatter_dimension=0, tiled=True)

    with jax.named_scope("unmix"):
        held_grad, g_scaled, r_scaled = call(
            unmix_kernel,
            (4,),
            [row_spec(quarter, span)] + [row_spec(quarter, width)] * 3,
            [whole(span, width), row_spec(quarter, width), row_spec(quarter, width)],
            [shaped(bf16, span, width)] * 3,
            2 * span * span * width,
            9e6,
            scratch=[pltpu.VMEM((span, width), f32)],
        )(*stay(expo, got_grad, inverse, mixed_held))
        got_values = swap_seq(held_grad.reshape(blocks, rows, width))

    with jax.named_scope("scores"):
        scores = call(
            scores_kernel,
            (4,),
            [row_spec(quarter, width), row_spec(quarter, width), whole(span, width)],
            row_spec(quarter, span),
            shaped(bf16, span, span),
            4 * span * span * width,
            8e6,
            scratch=[pltpu.VMEM((span, width), bf16)],
            prefetch=1,
        )(lengths, *stay(g_scaled, r_scaled, held))
        ffn_sum, scores, got_values = lax.optimization_barrier((ffn_sum, scores, got_values))
        scores = lax.psum_scatter(scores, "head", scatter_dimension=0, tiled=True)

    with jax.named_scope("ffn_sum"):
        piece = grad_rows // 8 // blocks
        ffn_sum = swap_seq(ffn_sum.reshape(blocks, piece, width // 2))
        ffn_sum = call(
            sum_spread_kernel,
            (1,),
            [whole(blocks, piece, width // 2)],
            whole(blocks, piece, width // 2),
            shaped(bf16, blocks, piece, width // 2),
            1e6,
            1e6,
        )(ffn_sum)
        ffn_sum = swap_seq(ffn_sum).reshape(grad_rows // 8, width // 2)
        ffn_sum = lax.all_gather(ffn_sum, "head", axis=0, tiled=True)

    with jax.named_scope("value_grad"):
        value_grad, value_part = call(
            value_grad_kernel,
            (steps,),
            [tok_spec(PER), move_spec(PER), whole(width)],
            [row_spec(tile, width), whole(128, 16, 128)],
            [shaped(bf16, total_rows, width), shaped(bf16, 128, 16, 128)],
            2 * total_rows * width * width,
            4e6,
            scratch=[pltpu.VMEM((width, width), f32)],
            prefetch=1,
        )(lengths, *stay(tokens), got_values, *stay(norm_gain))
        spread_all = call(
            sum_spread_kernel,
            (1,),
            [whole(128, 16, 128)],
            whole(128, 16, 128),
            shaped(bf16, 128, 16, 128),
            1e6,
            1e6,
        )
        value_sum = swap_all(spread_all(swap_all(value_part)))

    with jax.named_scope("input_grad"):
        input_grad = call(
            input_grad_kernel,
            (steps,),
            [
                tok_spec(PER),
                row_spec(tile, width),
                row_spec(tile, width),
                whole(width),
                whole(width, width),
            ],
            tok_spec(PER),
            shaped(f32, group, rows, width),
            2 * total_rows * width * width,
            7e6,
        )(*stay(tokens), value_grad, *stay(grad_resid, norm_gain, value_weight))

    with jax.named_scope("ffn_sum"):
        count = ff // width
        half_spec = pl.BlockSpec((width, width // 2), lambda q: (q, 0))
        down_grad, up_grad, out_grad, ffn_gain_grad = call(
            finish_ffn_kernel,
            (count,),
            [
                half_spec,
                pl.BlockSpec((width, width // 2), lambda q: (count + q, 0)),
                pl.BlockSpec((2 * width, width // 2), lambda q: (count + q, 0)),
                pl.BlockSpec((width, width // 2), lambda q: (4 * count, 0)),
                pl.BlockSpec((width, width // 2), lambda q: (4 * count + 1, 0)),
                pl.BlockSpec((width, width), lambda q: (0, q)),
                whole(width),
            ],
            [
                pl.BlockSpec((width, width), lambda q: (q, 0)),
                pl.BlockSpec((width, width), lambda q: (0, q)),
                whole(width, width),
                whole(1, width),
            ],
            [
                shaped(f32, ff, width),
                shaped(f32, width, ff),
                shaped(f32, width, width),
                shaped(f32, 1, width),
            ],
            4e6,
            13e6,
            scratch=[pltpu.VMEM((width, width), f32)],
        )(*stay(*[ffn_sum] * 5, up_weight, ffn_gain))

    with jax.named_scope("value_sum"):
        value_weight_grad, norm_gain_grad = call(
            finish_value_kernel,
            (1,),
            [whole(128, 16, 128), whole(width, width), whole(width)],
            [whole(width, width), whole(1, width)],
            [shaped(f32, width, width), shaped(f32, 1, width)],
            4e6,
            2e6,
        )(value_sum, *stay(value_weight, norm_gain))

    with jax.named_scope("logits_grad"):
        parts = scores.reshape(2, rows, span)
        low = y % 2
        part = at(parts, low).astype(f32) + flip(at(parts, 1 - low), y=1).astype(f32)
        part = to_plane(part.astype(bf16), back=True).astype(f32)
        logits = synth_logits.reshape(rows, span).astype(f32)
        exact = jnp.exp(logits - jnp.max(logits, axis=-1, keepdims=True))
        logits_grad = (part * exact).reshape(1, rows, span)
    return (
        output,
        input_grad,
        norm_gain_grad.reshape(width),
        value_weight_grad,
        logits_grad,
        out_grad,
        ffn_gain_grad.reshape(width),
        up_grad,
        down_grad,
    )


def solution(mesh):
    token_spec = P("head", "seq", None)
    placed = (
        token_spec,
        P(),
        P(),
        P(),
        token_spec,
        P(),
        P(),
        P(),
        P(),
        token_spec,
    )
    return jax.shard_map(
        shards,
        mesh=mesh,
        in_specs=placed,
        out_specs=(token_spec, token_spec, P(), P(), token_spec, P(), P(), P(), P()),
        check_vma=False,
    )
```

```python
import functools
import math

import jax
import jax.numpy as jnp
from jax import lax
from jax.experimental import pallas as pl
from jax.experimental.pallas import tpu as pltpu
from jax.sharding import PartitionSpec as P

EPS = 1e-06
ROOT_HALF = 1.0 / math.sqrt(2.0)
DENSITY = 1.0 / math.sqrt(2.0 * math.pi)
LANES = 128
CHUNK = 32
PER = LANES // CHUNK
PLANE = ("x", "y")
CHIPS = ("x", "y", "z")
ALL = ("x", "y", "z", "core")
bf16 = jnp.bfloat16
f32 = jnp.float32


def nt(left, right):
    return lax.dot_general(left, right, (((1,), (1,)), ((), ())), preferred_element_type=f32)


def tn(left, right):
    return lax.dot_general(left, right, (((0,), (0,)), ((), ())), preferred_element_type=f32)


def nn(left, right):
    return jnp.dot(left, right, preferred_element_type=f32)


def lane_groups(rows):
    return lax.broadcasted_iota(jnp.int32, (rows, LANES), 1) // CHUNK


def pick(groups, parts):
    out = parts[PER - 1]
    for l in range(PER - 2, -1, -1):
        out = jnp.where(groups == l, parts[l], out)
    return out


def seat(chunk):
    return chunk % 4 * 4 + chunk // 4


def spread(value, store):
    rows = value.shape[0] // PER
    groups = lane_groups(rows)
    for q in range(value.shape[1] // LANES):
        turned = []
        for r in range(PER):
            piece = value[r * rows : (r + 1) * rows, q * LANES : (q + 1) * LANES]
            turned.append(pltpu.roll(piece, CHUNK * r, 1) if r else piece)
        for k in range(PER):
            store(seat(q * PER + k), pick(groups, [turned[(l - k) % PER] for l in range(PER)]))


def collect(ref, group):
    chunks, rows, _ = ref.shape
    lanes = slice(group * LANES, (group + 1) * LANES)
    groups = lane_groups(rows)
    columns = []
    for q in range(chunks // PER):
        loaded = [ref[seat(q * PER + k), :, lanes].astype(f32) for k in range(PER)]
        parts = []
        for r in range(PER):
            mixed = pick(groups, [loaded[(l - r) % PER] for l in range(PER)])
            parts.append(pltpu.roll(mixed, LANES - CHUNK * r, 1) if r else mixed)
        columns.append(jnp.concatenate(parts, axis=0))
    return jnp.concatenate(columns, axis=1)


def places():
    return tuple(lax.axis_index(axis) for axis in ALL)


def first_bucket(lens_ref):
    _, _, z, c = places()
    return (z * 2 + c) * (lens_ref.shape[0] // 8)


def row_keep(lens_ref, buckets, rows):
    x, y, _, _ = places()
    spot = (x * 4 + y) * rows + lax.broadcasted_iota(jnp.int32, (rows, 1), 0)
    first = first_bucket(lens_ref) + pl.program_id(0) * buckets
    parts = [(spot < lens_ref[first + r]).astype(f32) for r in range(buckets)]
    return jnp.concatenate(parts, axis=0)


def gain_row(gain_ref):
    return gain_ref[...].astype(f32).reshape(1, gain_ref.shape[0])


def rms(values):
    scale = lax.rsqrt(jnp.mean(values * values, axis=-1, keepdims=True) + EPS)
    return values * scale, scale


def values_kernel(lens_ref, tok_ref, gain_ref, vw_ref, out_ref):
    per, rows, width = tok_ref.shape
    tok = tok_ref[...].reshape(per * rows, width).astype(f32)
    normed, _ = rms(tok)
    hidden = (normed * gain_row(gain_ref)).astype(bf16)
    val = nn(hidden, vw_ref[...]) * row_keep(lens_ref, per, rows)

    def store(chunk, block):
        out_ref[chunk] = block.astype(bf16)

    spread(val, store)


def lane_lengths(lens_ref, lanes):
    x, _, _, _ = places()
    group = lanes // CHUNK
    first = first_bucket(lens_ref)
    lane = lax.broadcasted_iota(jnp.int32, (1, lanes), 1) // CHUNK
    lens = jnp.zeros((1, lanes), jnp.int32)
    for n in range(group):
        m, l = divmod(n, PER)
        lens = jnp.where(lane == n, lens_ref[first + m * PER + (l - x + PER) % PER], lens)
    return lens


def mix_kernel(lens_ref, *refs):
    count = len(refs) - 12
    pieces = refs[:count]
    held_ref, exp_out, inv_out, mix_out = refs[count : count + 4]
    landed, held, keep, expo, inverse, mixed, sems, out_sems = refs[count + 4 :]
    span, lanes = held.shape
    x, _, z, c = places()
    half = pieces[0].shape[0] // 2
    copies = [
        pltpu.make_async_copy(piece, landed.at[n], sems.at[n]) for n, piece in enumerate(pieces)
    ]
    held_copy = pltpu.make_async_copy(held_ref, held, sems.at[count])
    copies[0].start()
    held_copy.start()
    for copy in copies[1:]:
        copy.start()
    lens = lane_lengths(lens_ref, lanes)
    place = lax.broadcasted_iota(jnp.int32, (span, lanes), 0)
    keep[...] = (place < lens).astype(f32).astype(bf16)
    out_copies = []
    deep = 4 * 2 * half
    for batch in range(2):
        starts = []
        bounds = []
        for n in range(4 * batch, 4 * batch + 4):
            copies[n].wait()
            core = c if batch == 0 else 1 - c
            ring = (z - n % 4 + 4) % 4
            for k in range(2):
                start = ((core * 2 + (x + k) % 2) * 4 + ring) * half
                starts.append(pl.multiple_of(start, half))
                bounds.append(lens - start)
        cut = pl.ds(4 * batch, 4)
        logits = landed[cut].reshape(deep, span).astype(f32)
        part = jnp.exp(logits - jnp.max(logits, axis=-1, keepdims=True)).astype(bf16)
        expo[cut] = part.reshape(4, 2 * half, span)
        totals = nn(part, keep[...])
        row = lax.broadcasted_iota(jnp.int32, (half, lanes), 0)
        kept = jnp.concatenate([(row < bound).astype(f32) for bound in bounds], axis=0)
        inverted = kept / totals
        inverse[cut] = inverted.reshape(4, 2 * half, lanes)
        if batch == 0:
            held_copy.wait()
        mixed[cut] = (nn(part, held[...]) * inverted).astype(bf16).reshape(4, 2 * half, lanes)
        for n in range(4 * batch, 4 * batch + 4):
            for j, (source, target) in enumerate(
                ((mixed, mix_out), (expo, exp_out), (inverse, inv_out))
            ):
                for k in range(2):
                    copy = pltpu.make_async_copy(
                        source.at[n, pl.ds(k * half, half), :],
                        target.at[pl.ds(starts[2 * (n - 4 * batch) + k], half), :],
                        out_sems.at[n, j, k],
                    )
                    copy.start()
                    out_copies.append(copy)
    for copy in out_copies:
        copy.wait()


def unmix_kernel(exp_ref, gm_ref, inv_ref, mixed_ref, out_ref, g_ref, r_ref):
    @pl.when(pl.program_id(0) == 0)
    def _():
        scaled = gm_ref[...].astype(f32) * inv_ref[...]
        g_ref[...] = scaled.astype(bf16)
        r_ref[...] = (scaled * mixed_ref[...].astype(f32)).astype(bf16)

    out_ref[...] = tn(exp_ref[...], g_ref[...]).astype(bf16)


def scores_kernel(lens_ref, g_ref, r_ref, val_ref, own_ref, other_ref, keep_ref):
    span, lanes = val_ref.shape

    @pl.when(pl.program_id(0) == 0)
    def _():
        place = lax.broadcasted_iota(jnp.int32, (span, lanes), 0)
        keep_ref[...] = (place < lane_lengths(lens_ref, lanes)).astype(f32).astype(bf16)

    out = (nt(g_ref[...], val_ref[...]) - nt(r_ref[...], keep_ref[...])).astype(bf16)
    step = pl.program_id(0)
    _, _, _, c = places()
    rings, _, rows, _ = own_ref.shape

    def store(ref):
        for n in range(rings):
            ref[n, step % 2] = out[n * rows : (n + 1) * rows]

    @pl.when(step // 2 == c)
    def _():
        store(own_ref)

    @pl.when(step // 2 != c)
    def _():
        store(other_ref)


def ffn_kernel(
    lens_ref,
    tok_ref,
    cot_ref,
    mix_ref,
    ow_ref,
    gain_ref,
    up_ref,
    down_ref,
    out_ref,
    gr_ref,
    gm_ref,
    own_out,
    other_out,
    down_acc,
    up_acc,
    ow_acc,
):
    per, rows, width = tok_ref.shape
    n = per * rows
    ff = up_ref.shape[1]
    step = up_acc.shape[2]

    @pl.when(pl.program_id(0) == 0)
    def _():
        down_acc[...] = jnp.zeros_like(down_acc)
        up_acc[...] = jnp.zeros_like(up_acc)
        ow_acc[...] = jnp.zeros_like(ow_acc)

    keep = row_keep(lens_ref, per, rows)
    tok = tok_ref[...].reshape(n, width).astype(f32)
    grad_low = (cot_ref[...].reshape(n, width).astype(f32) * keep).astype(bf16)
    mixed = jnp.concatenate(
        [collect(mix_ref, g) for g in range(per // PER)], axis=0
    ).astype(bf16)
    resid = tok + nn(mixed, ow_ref[...])
    normed, scale = rms(resid)
    gain = gain_row(gain_ref)
    hidden = (normed * gain).astype(bf16)
    ffn = jnp.zeros((n, width), f32)
    grad_hidden = jnp.zeros((n, width), f32)
    for q in range(ff // step):
        cut = slice(q * step, (q + 1) * step)
        up = up_ref[:, cut]
        down = down_ref[cut, :]
        pre = nn(hidden, up)
        cdf = 0.5 * (1.0 + lax.erf(pre * ROOT_HALF))
        slope = cdf + pre * jnp.exp(-0.5 * pre * pre) * DENSITY
        act = (pre * cdf).astype(bf16)
        ffn = ffn + nn(act, down)
        grad_pre = (nt(grad_low, down) * slope).astype(bf16)
        grad_hidden = grad_hidden + nt(grad_pre, up)
        down_acc[cut, :] += tn(act, grad_low)
        up_acc[q] += tn(hidden, grad_pre)
    out_ref[...] = ((resid + ffn) * keep).astype(bf16).reshape(per, rows, width)
    weighted = grad_hidden * gain
    back = scale * (weighted - normed * jnp.mean(weighted * normed, axis=-1, keepdims=True))
    grad_resid = grad_low.astype(f32) + back
    gr_ref[...] = grad_resid
    grad_att = grad_resid.astype(bf16)
    ow_acc[...] += tn(mixed, grad_att)
    grad_mixed = nt(grad_att, ow_ref[...]) * keep
    size = PER * rows
    for g in range(per // PER):

        def store(chunk, block, g=g):
            gm_ref[chunk, :, g * LANES : (g + 1) * LANES] = block.astype(bf16)

        spread(grad_mixed[g * size : (g + 1) * size], store)

    @pl.when(pl.program_id(0) == pl.num_programs(0) - 1)
    def _():
        _, _, _, core = places()
        half = width // 2
        count, tall, _ = own_out.shape
        deep = tall - 2 * width
        for ref, side in ((other_out, 1 - core), (own_out, core)):
            lanes = pl.ds(pl.multiple_of(side * half, half), half)
            for n in range(count):
                ref[n, :width, :] = down_acc[n * width : (n + 1) * width, lanes].astype(bf16)
                ref[n, width : 2 * width, :] = up_acc[n, :, lanes].astype(bf16)
                ref[n, 2 * width :, :] = ow_acc[n * deep : (n + 1) * deep, lanes].astype(bf16)


def value_grad_kernel(lens_ref, tok_ref, vg_ref, gain_ref, ffn_ref, vgrad_ref, joint_ref, acc_ref):
    per, rows, width = tok_ref.shape
    tok = tok_ref[...].reshape(per * rows, width).astype(f32)
    normed, _ = rms(tok)
    hidden = (normed * gain_row(gain_ref)).astype(bf16)
    vgrad = (collect(vg_ref, 0) * row_keep(lens_ref, per, rows)).astype(bf16)
    vgrad_ref[...] = vgrad

    @pl.when(pl.program_id(0) == 0)
    def _():
        acc_ref[...] = jnp.zeros_like(acc_ref)

    acc_ref[...] += tn(hidden, vgrad)

    @pl.when(pl.program_id(0) == pl.num_programs(0) - 1)
    def _():
        count, tall, half = joint_ref.shape
        deep = ffn_ref.shape[1]
        rows_here = (tall - deep) // 2
        joint_ref[:, :deep, :] = ffn_ref[...]
        for n in range(count):
            for k in range(2):
                joint_ref[n, deep + k * rows_here : deep + (k + 1) * rows_here, :] = acc_ref[
                    n * rows_here : (n + 1) * rows_here, k * half : (k + 1) * half
                ].astype(bf16)


def input_grad_kernel(tok_ref, vgrad_ref, gr_ref, gain_ref, vw_ref, out_ref):
    per, rows, width = tok_ref.shape
    tok = tok_ref[...].reshape(per * rows, width).astype(f32)
    normed, scale = rms(tok)
    weighted = nt(vgrad_ref[...], vw_ref[...]) * gain_row(gain_ref)
    back = scale * (weighted - normed * jnp.mean(weighted * normed, axis=-1, keepdims=True))
    out_ref[...] = (gr_ref[...] + back).reshape(per, rows, width)


def joint_sum_kernel(joint_ref, ffn_ref, value_ref):
    total = jnp.sum(joint_ref[...].astype(f32), axis=0).astype(bf16)
    deep = ffn_ref.shape[1]
    ffn_ref[...] = jnp.broadcast_to(total[None, :deep], ffn_ref.shape)
    value_ref[...] = total[deep:]


def ring_spread_kernel(*refs):
    parts, out_ref, held = refs[:4], refs[4], refs[5]
    me = lax.axis_index("z")
    for k, part in enumerate(parts):
        held[(me - k + 4) % 4] = part[...].astype(f32)
    total = (held[0] + held[1]) + (held[2] + held[3])
    out_ref[...] = jnp.broadcast_to(total[None], out_ref.shape).astype(bf16)


def row_total(product):
    folded = sum(
        product[:, n * LANES : (n + 1) * LANES] for n in range(product.shape[1] // LANES)
    )
    return jnp.sum(folded.T, axis=0, keepdims=True)


def fold_kernel(own_ref, got_ref, *outs):
    step = pl.program_id(0)
    total = (own_ref[0].astype(f32) + got_ref[0].astype(f32)).astype(bf16)
    for k, out in enumerate(outs):

        @pl.when(step == k)
        def _(out=out):
            out[...] = total


def sum_kernel(*refs):
    parts, out_ref = refs[:-1], refs[-1]
    out_ref[...] = sum(part[...].astype(f32) for part in parts).astype(bf16)


def split_sum_kernel(*refs):
    parts, (own_ref, other_ref) = refs[:4], refs[4:]
    total = sum(part[...].astype(f32) for part in parts).astype(bf16)
    odd = places()[0] % 2 == 1
    own_ref[...] = jnp.where(odd, total[1], total[0])
    other_ref[...] = jnp.where(odd, total[0], total[1])


def logits_grad_kernel(part_ref, logits_ref, out_ref):
    logits = logits_ref[0].astype(f32)
    exact = jnp.exp(logits - jnp.max(logits, axis=-1, keepdims=True))
    out_ref[0] = part_ref[...].astype(f32) * exact


def finish_ffn_kernel(*refs):
    pieces, (up_ref, gain_ref), (down_out, up_out, ow_out, gain_out) = refs[:8], refs[8:10], refs[10:14]
    landed, wide, up, sems, out_sems = refs[14:]
    width = up.shape[0]
    half = landed.shape[2]
    deep = landed.shape[1] - 2 * width
    _, _, z, c = places()
    copies = [
        pltpu.make_async_copy(piece, landed.at[n], sems.at[n]) for n, piece in enumerate(pieces)
    ]
    up_copy = pltpu.make_async_copy(up_ref, up, sems.at[8])
    copies[0].start()
    up_copy.start()
    for copy in copies[1:]:
        copy.start()
    product = jnp.zeros((width, half), f32)
    out_copies = []
    for n, copy in enumerate(copies):
        copy.wait()
        ring = (z - n % 4 + 4) % 4
        side = c if n < 4 else 1 - c
        wide[n] = landed[n].astype(f32)
        lanes = pl.ds(pl.multiple_of(side * half, half), half)
        columns = pl.ds(pl.multiple_of((2 * ring + side) * half, half), half)
        targets = (
            (0, width, down_out.at[pl.ds(pl.multiple_of(ring * width, width), width), lanes]),
            (width, width, up_out.at[:, columns]),
            (2 * width, deep, ow_out.at[pl.ds(pl.multiple_of(ring * deep, deep), deep), lanes]),
        )
        for k, (first, tall, target) in enumerate(targets):
            out_copy = pltpu.make_async_copy(
                wide.at[n, pl.ds(first, tall), :], target, out_sems.at[n, k]
            )
            out_copy.start()
            out_copies.append(out_copy)
        if n == 0:
            up_copy.wait()
        product = product + up[:, columns].astype(f32) * wide[n, width : 2 * width, :]
    gain_out[...] = row_total(product) / gain_row(gain_ref)
    for out_copy in out_copies:
        out_copy.wait()


def finish_value_kernel(in_ref, vw_ref, gain_ref, out_ref, gain_out):
    count, tall, half = in_ref.shape
    rows_here = tall // 2
    for n in range(count):
        for k in range(2):
            out_ref[n * rows_here : (n + 1) * rows_here, k * half : (k + 1) * half] = in_ref[
                n, k * rows_here : (k + 1) * rows_here
            ].astype(f32)
    gain_out[...] = row_total(vw_ref[...].astype(f32) * out_ref[...]) / gain_row(gain_ref)


def params():
    return pltpu.CompilerParams(vmem_limit_bytes=63 * 1024 * 1024)


def cost(flops, size):
    return pl.CostEstimate(flops=int(flops), bytes_accessed=int(size), transcendentals=0)


def whole(*shape):
    return pl.BlockSpec(shape, lambda *_: (0,) * len(shape))


def once(*shape):
    return pl.BlockSpec(shape, lambda *_: (0,) * len(shape), pipeline_mode=pl.Buffered(1))


def shaped(dtype, *shape):
    return pltpu.HBM(shape, dtype)


def stay(*arrays):
    return [pltpu.with_memory_space_constraint(array, pltpu.HBM) for array in arrays]


def flat(x, y, z, c):
    return ((x % 4) * 4 + y % 4) * 8 + (z % 4) * 2 + c % 2


def devices():
    for i in range(128):
        s, h = divmod(i, 8)
        yield i, s // 4, s % 4, h // 2, h % 2


def shift(array, axis, step):
    return lax.ppermute(array, axis, [(i, (i + step) % 4) for i in range(4)])


def flip(array):
    return lax.ppermute(array, "core", [(0, 1), (1, 0)])


def flip_x(array):
    return lax.ppermute(array, "x", [(i, i ^ 1) for i in range(4)])


def to_plane(array, back=False):
    pairs = [(i, flat(2 * e + (a & 1), d, b, a >> 1)) for i, a, b, d, e in devices()]
    if back:
        pairs = [(j, i) for i, j in pairs]
    return lax.ppermute(array, ALL, pairs)


def around(parts, axis):
    return [parts[0]] + [shift(parts[step], axis, step) for step in (1, 2, 3)]


def swap(array, axes):
    return lax.all_to_all(array, axes, 0, 0, tiled=True)


def swap_seq(array):
    return swap(array, PLANE)


def after(array, *others):
    return lax.optimization_barrier((array,) + others)[0]


def ordered(arrays, *others):
    return list(lax.optimization_barrier((*arrays, *others)))[: len(arrays)]


def shards(
    tokens,
    lengths,
    norm_gain,
    value_weight,
    synth_logits,
    out_weight,
    ffn_gain,
    up_weight,
    down_weight,
    cotangent,
):
    group, rows, width = tokens.shape
    span = synth_logits.shape[2]
    ff = up_weight.shape[1]
    blocks = span // rows
    total_rows = group * rows
    steps = group // PER
    tile = PER * rows

    def tok_spec(n):
        return pl.BlockSpec((n, rows, width), lambda m, *_: (m, 0, 0))

    def move_spec(n):
        return pl.BlockSpec((blocks, rows, n // PER * LANES), lambda m, *_: (0, 0, m))

    def row_spec(n, columns):
        return pl.BlockSpec((n, columns), lambda m, *_: (m, 0))

    def call(kernel, grid, ins, outs, shapes, flops, size, scratch=(), prefetch=0, long=False):
        return pl.pallas_call(
            kernel,
            grid_spec=pltpu.PrefetchScalarGridSpec(
                num_scalar_prefetch=prefetch,
                grid=grid,
                in_specs=ins,
                out_specs=outs,
                scratch_shapes=scratch,
            ),
            out_shape=shapes,
            compiler_params=params(),
            cost_estimate=cost(1e13, 1e6) if long else cost(1e6, 1e5),
        )

    with jax.named_scope("logits"):
        block = synth_logits.reshape(rows, span)
        block = to_plane(block)

    with jax.named_scope("values"):
        sent_values = call(
            values_kernel,
            (steps,),
            [tok_spec(PER), whole(width), whole(width, width)],
            move_spec(PER),
            shaped(bf16, blocks, rows, width),
            2 * total_rows * width * width,
            3e6,
            prefetch=1,
        )(lengths, *stay(tokens, norm_gain, value_weight))
        block = ordered([block], sent_values)[0]

    with jax.named_scope("logits"):
        other = flip_x(block)
        pair = jnp.concatenate([block, other])
        held = swap_seq(ordered([sent_values], other)[0]).reshape(span, width)
        pieces = [pair] + [shift(pair, "z", step) for step in (1, 2, 3)]
        pieces = pieces + [flip(piece) for piece in pieces]

    quarter = span // 4
    anywhere = pl.BlockSpec(memory_space=pl.ANY)
    with jax.named_scope("mix"):
        expo, inverse, mixed_held = call(
            mix_kernel,
            (1,),
            [anywhere] * 9,
            [anywhere] * 3,
            [shaped(bf16, span, span), shaped(f32, span, width), shaped(bf16, span, width)],
            4 * span * span * width,
            8e6,
            scratch=[
                pltpu.VMEM((8, 2 * rows, span), bf16),
                pltpu.VMEM((span, width), bf16),
                pltpu.VMEM((span, width), bf16),
                pltpu.VMEM((8, 2 * rows, span), bf16),
                pltpu.VMEM((8, 2 * rows, width), f32),
                pltpu.VMEM((8, 2 * rows, width), bf16),
                pltpu.SemaphoreType.DMA((9,)),
                pltpu.SemaphoreType.DMA((8, 3, 2)),
            ],
            prefetch=1,
        )(lengths, *pieces, held)
        got_mixed = swap_seq(mixed_held.reshape(blocks, rows, width))

    tall = ff // 4 + width + width // 4
    half_width = width // 2
    grads_shape = (4, tall, half_width)
    with jax.named_scope("ffn"):
        output, grad_resid, sent_grad, own_part, other_part = call(
            ffn_kernel,
            (steps // 2,),
            [
                tok_spec(2 * PER),
                tok_spec(2 * PER),
                move_spec(2 * PER),
                once(width, width),
                once(width),
                once(width, ff),
                once(ff, width),
            ],
            [
                tok_spec(2 * PER),
                row_spec(2 * tile, width),
                move_spec(2 * PER),
                once(*grads_shape),
                once(*grads_shape),
            ],
            [
                shaped(bf16, group, rows, width),
                shaped(f32, total_rows, width),
                shaped(bf16, blocks, rows, width),
                shaped(bf16, *grads_shape),
                shaped(bf16, *grads_shape),
            ],
            2 * total_rows * width * (6 * ff + 3 * width),
            2e7,
            scratch=[
                pltpu.VMEM((ff, width), f32),
                pltpu.VMEM((ff // width, width, width), f32),
                pltpu.VMEM((width, width), f32),
            ],
            prefetch=1,
        )(
            lengths,
            *stay(tokens, cotangent), got_mixed, *stay(out_weight, ffn_gain, up_weight, down_weight),
        )
        got_grad = swap_seq(sent_grad).reshape(span, width)

    def fold(own, got):
        shape = own.shape[1:]
        zeros = (0,) * len(shape)
        part = pl.BlockSpec((1,) + shape, lambda k: ((lax.axis_index("z") + k) % 4,) + zeros)
        return call(
            fold_kernel,
            (4,),
            [part] * 2,
            [whole(*shape)] * 4,
            [shaped(bf16, *shape)] * 4,
            1e6,
            6 * math.prod(own.shape),
        )(*stay(own), got)

    with jax.named_scope("ffn_sum"):
        folded = fold(own_part, flip(other_part))
        ring_parts = around(folded, "z")
        got_grad = ordered([got_grad], folded[0])[0]

    with jax.named_scope("unmix"):
        held_grad, g_scaled, r_scaled = call(
            unmix_kernel,
            (4,),
            [pl.BlockSpec((span, quarter), lambda j: (0, j))] + [once(span, width)] * 3,
            [row_spec(quarter, width), whole(span, width), whole(span, width)],
            [shaped(bf16, span, width)] * 3,
            2 * span * span * width,
            9e6,
        )(*stay(expo), got_grad, *stay(inverse, mixed_held))
        got_values = swap_seq(held_grad.reshape(blocks, rows, width))


    with jax.named_scope("scores"):
        score_shape = (4, 2, rows, span)
        own_scores, other_scores = call(
            scores_kernel,
            (4,),
            [row_spec(quarter, width), row_spec(quarter, width), whole(span, width)],
            [whole(*score_shape)] * 2,
            [shaped(bf16, *score_shape)] * 2,
            4 * span * span * width,
            8e6,
            scratch=[pltpu.VMEM((span, width), bf16)],
            prefetch=1,
        )(lengths, *stay(g_scaled, r_scaled), ordered([held], held_grad)[0])
        got_scores = flip(other_scores)

    with jax.named_scope("ffn_sum"):
        part = row_spec(tall // 4, half_width)
        ring_parts = ordered(ring_parts, own_scores)
        ffn_sum = call(
            sum_kernel,
            (4,),
            [part] * 4,
            part,
            shaped(bf16, tall, half_width),
            1e6,
            3e6,
            long=True,
        )(*ring_parts)

    with jax.named_scope("score_sum"):
        score_parts = fold(*ordered([own_scores, got_scores], ffn_sum))
        score_ring = around(score_parts, "z")
        got_values = ordered([got_values], score_parts[0])[0]

    with jax.named_scope("ffn_sum"):
        piece = tall // blocks
        ffn_sum = ffn_sum.reshape(blocks, piece, half_width)
        joint = piece + 2 * (width // blocks)

    with jax.named_scope("value_grad"):
        value_grad, joint_part = call(
            value_grad_kernel,
            (steps,),
            [tok_spec(PER), move_spec(PER), whole(width), whole(blocks, piece, half_width)],
            [row_spec(tile, width), whole(blocks, joint, half_width)],
            [shaped(bf16, total_rows, width), shaped(bf16, blocks, joint, half_width)],
            2 * total_rows * width * width,
            4e6,
            scratch=[pltpu.VMEM((width, width), f32)],
            prefetch=1,
        )(lengths, *stay(tokens), got_values, *stay(norm_gain), ffn_sum)
        got_joint = swap_seq(joint_part)

    with jax.named_scope("score_sum"):
        own_scores, other_scores = call(
            split_sum_kernel,
            (1,),
            [whole(2, rows, span)] * 4,
            [whole(rows, span)] * 2,
            [shaped(bf16, rows, span)] * 2,
            1e6,
            2e6,
            long=True,
        )(*ordered(score_ring, joint_part))
        got_scores = flip_x(other_scores)

    with jax.named_scope("input_grad"):
        input_grad = call(
            input_grad_kernel,
            (steps,),
            [
                tok_spec(PER),
                row_spec(tile, width),
                row_spec(tile, width),
                whole(width),
                whole(width, width),
            ],
            tok_spec(PER),
            shaped(f32, group, rows, width),
            2 * total_rows * width * width,
            7e6,
        )(*stay(tokens), value_grad, *stay(*ordered([grad_resid], own_scores), norm_gain, value_weight))

    with jax.named_scope("score_sum"):
        score_total = call(
            sum_kernel,
            (1,),
            [whole(rows, span)] * 2,
            whole(rows, span),
            shaped(bf16, rows, span),
            1e6,
            1e6,
        )(*ordered([own_scores, got_scores], input_grad))
        score_back = to_plane(score_total, back=True)

    with jax.named_scope("joint_sum"):
        few = (joint - piece, half_width)
        ffn_spread, small = call(
            joint_sum_kernel,
            (1,),
            [whole(blocks, joint, half_width)],
            [whole(blocks, piece, half_width), whole(*few)],
            [shaped(bf16, blocks, piece, half_width), shaped(bf16, *few)],
            1e6,
            2e6,
        )(*ordered([got_joint], score_total))

    with jax.named_scope("value_sum"):
        small = call(
            sum_kernel,
            (1,),
            [whole(*few)] * 2,
            whole(*few),
            shaped(bf16, *few),
            1e6,
            1e6,
        )(small, flip(small))
        value_spread = call(
            ring_spread_kernel,
            (1,),
            [whole(*few)] * 4,
            whole(blocks, *few),
            shaped(bf16, blocks, *few),
            1e6,
            1e6,
            scratch=[pltpu.VMEM((4, *few), f32)],
        )(*around([small] * 4, "z"))

    with jax.named_scope("score_sum"):
        logits_grad = call(
            logits_grad_kernel,
            (1,),
            [whole(rows, span), whole(1, rows, span)],
            whole(1, rows, span),
            shaped(f32, 1, rows, span),
            1e6,
            1e6,
        )(*ordered([score_back], value_spread), synth_logits)

    with jax.named_scope("ffn_sum"):
        ffn_sum = ordered([swap_seq(ffn_spread)], value_spread)[0].reshape(tall, half_width)
        pieces = around([ffn_sum] * 4, "z")

    with jax.named_scope("value_sum"):
        value_sum = swap_seq(ordered([value_spread], ffn_sum)[0])

    with jax.named_scope("value_sum"):
        value_weight_grad, norm_gain_grad = call(
            finish_value_kernel,
            (1,),
            [whole(blocks, *few), whole(width, width), whole(width)],
            [whole(width, width), whole(1, width)],
            [shaped(f32, width, width), shaped(f32, 1, width)],
            4e6,
            2e6,
        )(value_sum, *stay(value_weight, norm_gain))

    with jax.named_scope("ffn_sum"):
        pieces = ordered(pieces, value_weight_grad, logits_grad)
        pieces = pieces + [flip(part) for part in pieces]
        down_grad, up_grad, out_grad, ffn_gain_grad = call(
            finish_ffn_kernel,
            (1,),
            [anywhere] * 9 + [whole(width)],
            [anywhere] * 3 + [whole(1, width)],
            [
                shaped(f32, ff, width),
                shaped(f32, width, ff),
                shaped(f32, width, width),
                shaped(f32, 1, width),
            ],
            4e6,
            13e6,
            scratch=[
                pltpu.VMEM((8, tall, half_width), bf16),
                pltpu.VMEM((8, tall, half_width), f32),
                pltpu.VMEM((width, ff), bf16),
                pltpu.SemaphoreType.DMA((9,)),
                pltpu.SemaphoreType.DMA((8, 3)),
            ],
        )(*pieces, *stay(up_weight, ffn_gain))

    return (
        output,
        input_grad,
        norm_gain_grad.reshape(width),
        value_weight_grad,
        logits_grad,
        out_grad,
        ffn_gain_grad.reshape(width),
        up_grad,
        down_grad,
    )


def solution(mesh):
    token_spec = P(("z", "core"), PLANE, None)
    placed = (
        token_spec,
        P(),
        P(),
        P(),
        token_spec,
        P(),
        P(),
        P(),
        P(),
        token_spec,
    )
    fine = jax.sharding.Mesh(mesh.devices.reshape(4, 4, 4, 2), ALL)
    return jax.shard_map(
        shards,
        mesh=fine,
        in_specs=placed,
        out_specs=(token_spec, token_spec, P(), P(), token_spec, P(), P(), P(), P()),
        check_vma=False,
    )
```

```python
import functools
import math

import jax
import jax.numpy as jnp
from jax import lax
from jax.experimental import pallas as pl
from jax.experimental.pallas import tpu as pltpu
from jax.sharding import PartitionSpec as P

EPS = 1e-06
ROOT_HALF = 1.0 / math.sqrt(2.0)
DENSITY = 1.0 / math.sqrt(2.0 * math.pi)
LANES = 128
CHUNK = 32
PER = LANES // CHUNK
PLANE = ("x", "y")
CHIPS = ("x", "y", "z")
ALL = ("x", "y", "z", "core")
bf16 = jnp.bfloat16
f32 = jnp.float32


def nt(left, right):
    return lax.dot_general(left, right, (((1,), (1,)), ((), ())), preferred_element_type=f32)


def tn(left, right):
    return lax.dot_general(left, right, (((0,), (0,)), ((), ())), preferred_element_type=f32)


def nn(left, right):
    return jnp.dot(left, right, preferred_element_type=f32)


def lane_groups(rows):
    return lax.broadcasted_iota(jnp.int32, (rows, LANES), 1) // CHUNK


def pick(groups, parts):
    out = parts[PER - 1]
    for l in range(PER - 2, -1, -1):
        out = jnp.where(groups == l, parts[l], out)
    return out


def seat(chunk):
    return chunk % 4 * 4 + chunk // 4


def spread(value, store):
    rows = value.shape[0] // PER
    groups = lane_groups(rows)
    for q in range(value.shape[1] // LANES):
        turned = []
        for r in range(PER):
            piece = value[r * rows : (r + 1) * rows, q * LANES : (q + 1) * LANES]
            turned.append(pltpu.roll(piece, CHUNK * r, 1) if r else piece)
        for k in range(PER):
            store(seat(q * PER + k), pick(groups, [turned[(l - k) % PER] for l in range(PER)]))


def collect(ref, group):
    chunks, rows, _ = ref.shape
    lanes = slice(group * LANES, (group + 1) * LANES)
    groups = lane_groups(rows)
    columns = []
    for q in range(chunks // PER):
        loaded = [ref[seat(q * PER + k), :, lanes].astype(f32) for k in range(PER)]
        parts = []
        for r in range(PER):
            mixed = pick(groups, [loaded[(l - r) % PER] for l in range(PER)])
            parts.append(pltpu.roll(mixed, LANES - CHUNK * r, 1) if r else mixed)
        columns.append(jnp.concatenate(parts, axis=0))
    return jnp.concatenate(columns, axis=1)


def places():
    return tuple(lax.axis_index(axis) for axis in ALL)


def first_bucket(lens_ref):
    _, _, z, c = places()
    return (z * 2 + c) * (lens_ref.shape[0] // 8)


def row_keep(lens_ref, buckets, rows):
    x, y, _, _ = places()
    spot = (x * 4 + y) * rows + lax.broadcasted_iota(jnp.int32, (rows, 1), 0)
    first = first_bucket(lens_ref) + pl.program_id(0) * buckets
    parts = [(spot < lens_ref[first + r]).astype(f32) for r in range(buckets)]
    return jnp.concatenate(parts, axis=0)


def gain_row(gain_ref):
    return gain_ref[...].astype(f32).reshape(1, gain_ref.shape[0])


def rms(values):
    scale = lax.rsqrt(jnp.mean(values * values, axis=-1, keepdims=True) + EPS)
    return values * scale, scale


def values_kernel(lens_ref, tok_ref, gain_ref, vw_ref, out_ref):
    per, rows, width = tok_ref.shape
    tok = tok_ref[...].reshape(per * rows, width).astype(f32)
    normed, _ = rms(tok)
    hidden = (normed * gain_row(gain_ref)).astype(bf16)
    val = nn(hidden, vw_ref[...]) * row_keep(lens_ref, per, rows)

    size = PER * rows
    for g in range(per // PER):

        def store(chunk, block, g=g):
            out_ref[chunk, :, g * LANES : (g + 1) * LANES] = block.astype(bf16)

        spread(val[g * size : (g + 1) * size], store)


def lane_lengths(lens_ref, lanes):
    x, _, _, _ = places()
    group = lanes // CHUNK
    first = first_bucket(lens_ref)
    lane = lax.broadcasted_iota(jnp.int32, (1, lanes), 1) // CHUNK
    lens = jnp.zeros((1, lanes), jnp.int32)
    for n in range(group):
        m, l = divmod(n, PER)
        lens = jnp.where(lane == n, lens_ref[first + m * PER + (l - x + PER) % PER], lens)
    return lens


def mix_kernel(lens_ref, *refs):
    count = len(refs) - 12
    pieces = refs[:count]
    held_ref, exp_out, inv_out, mix_out = refs[count : count + 4]
    landed, held, keep, expo, inverse, mixed, sems, out_sems = refs[count + 4 :]
    span, lanes = held.shape
    x, _, z, c = places()
    half = pieces[0].shape[0] // 2
    copies = [
        pltpu.make_async_copy(piece, landed.at[n], sems.at[n]) for n, piece in enumerate(pieces)
    ]
    held_copy = pltpu.make_async_copy(held_ref, held, sems.at[count])
    copies[0].start()
    held_copy.start()
    for copy in copies[1:]:
        copy.start()
    lens = lane_lengths(lens_ref, lanes)
    place = lax.broadcasted_iota(jnp.int32, (span, lanes), 0)
    keep[...] = (place < lens).astype(f32).astype(bf16)
    out_copies = []
    deep = 4 * 2 * half
    for batch in range(2):
        starts = []
        bounds = []
        for n in range(4 * batch, 4 * batch + 4):
            copies[n].wait()
            core = c if batch == 0 else 1 - c
            ring = (z - n % 4 + 4) % 4
            for k in range(2):
                start = ((core * 2 + (x + k) % 2) * 4 + ring) * half
                starts.append(pl.multiple_of(start, half))
                bounds.append(lens - start)
        cut = pl.ds(4 * batch, 4)
        logits = landed[cut].reshape(deep, span).astype(f32)
        part = jnp.exp(logits - jnp.max(logits, axis=-1, keepdims=True)).astype(bf16)
        expo[cut] = part.reshape(4, 2 * half, span)
        totals = nn(part, keep[...])
        row = lax.broadcasted_iota(jnp.int32, (half, lanes), 0)
        kept = jnp.concatenate([(row < bound).astype(f32) for bound in bounds], axis=0)
        inverted = kept / totals
        inverse[cut] = inverted.reshape(4, 2 * half, lanes)
        if batch == 0:
            held_copy.wait()
        mixed[cut] = (nn(part, held[...]) * inverted).astype(bf16).reshape(4, 2 * half, lanes)
        for n in range(4 * batch, 4 * batch + 4):
            for j, (source, target) in enumerate(
                ((mixed, mix_out), (expo, exp_out), (inverse, inv_out))
            ):
                for k in range(2):
                    copy = pltpu.make_async_copy(
                        source.at[n, pl.ds(k * half, half), :],
                        target.at[pl.ds(starts[2 * (n - 4 * batch) + k], half), :],
                        out_sems.at[n, j, k],
                    )
                    copy.start()
                    out_copies.append(copy)
    for copy in out_copies:
        copy.wait()


def unmix_kernel(exp_ref, gm_ref, inv_ref, mixed_ref, out_ref, g_ref, r_ref):
    @pl.when(pl.program_id(0) == 0)
    def _():
        scaled = gm_ref[...].astype(f32) * inv_ref[...]
        g_ref[...] = scaled.astype(bf16)
        r_ref[...] = (scaled * mixed_ref[...].astype(f32)).astype(bf16)

    out_ref[...] = tn(exp_ref[...], g_ref[...]).astype(bf16)


def scores_kernel(lens_ref, g_ref, r_ref, val_ref, own_ref, other_ref, keep_ref):
    span, lanes = val_ref.shape

    @pl.when(pl.program_id(0) == 0)
    def _():
        place = lax.broadcasted_iota(jnp.int32, (span, lanes), 0)
        keep_ref[...] = (place < lane_lengths(lens_ref, lanes)).astype(f32).astype(bf16)

    out = (nt(g_ref[...], val_ref[...]) - nt(r_ref[...], keep_ref[...])).astype(bf16)
    step = pl.program_id(0)
    _, _, _, c = places()
    rings, bits, rows, _ = own_ref.shape

    def store(ref):
        for bit in range(bits):
            for n in range(rings):
                first = (bit * rings + n) * rows
                ref[n, bit] = out[first : first + rows]

    @pl.when(step == c)
    def _():
        store(own_ref)

    @pl.when(step != c)
    def _():
        store(other_ref)


def ffn_kernel(lens_ref, *refs):
    ins, refs = refs[:7], refs[7:]
    tok_in, cot_in, mix_in, ow_in, gain_ref, up_in, down_in = ins
    out_ref, gr_ref, gm_ref, own_ref, other_ref = refs[:5]
    tok_v, cot_v, mix_v, ow_v, up_v, down_v, out_v, gr_v, gm_v, own_v, other_v, grad_v = refs[5:17]
    sems, out_sems = refs[17:]
    per, rows, width = tok_v.shape
    n = per * rows
    ff = up_v.shape[1]
    step = width
    _, _, _, core = places()
    half = width // 2
    deep = own_v.shape[1] - 2 * width

    def fetch(k, source, target):
        copy = pltpu.make_async_copy(source, target, sems.at[k])
        copy.start()
        return copy

    mix_copy = fetch(0, mix_in, mix_v)
    ow_copy = fetch(1, ow_in, ow_v)
    tok_copy = fetch(2, tok_in, tok_v)
    up_copy = fetch(3, up_in, up_v)
    cot_copy = fetch(4, cot_in, cot_v)
    down_copy = fetch(5, down_in, down_v)
    sent = []

    def send(source, target):
        copy = pltpu.make_async_copy(source, target, out_sems.at[len(sent)])
        copy.start()
        sent.append(copy)

    keep = row_keep(lens_ref, per, rows)
    mix_copy.wait()
    mixed = jnp.concatenate([collect(mix_v, g) for g in range(per // PER)], axis=0).astype(bf16)
    ow_copy.wait()
    tok_copy.wait()
    resid = tok_v[...].reshape(n, width).astype(f32) + nn(mixed, ow_v[...])
    normed, scale = rms(resid)
    gain = gain_row(gain_ref)
    hidden = (normed * gain).astype(bf16)
    cot_copy.wait()
    grad_low = (cot_v[...].reshape(n, width).astype(f32) * keep).astype(bf16)
    up_copy.wait()

    def add(ref, spot, side, source):
        lanes = pl.ds(pl.multiple_of(side * half, half), half)
        ref[spot] = grad_v[source, lanes].astype(bf16)

    def split(spot, source):
        add(other_v, spot, 1 - core, source)
        add(own_v, spot, core, source)

    ffn = jnp.zeros((n, width), f32)
    grad_hidden = jnp.zeros((n, width), f32)
    everything = slice(0, width)
    for q in range(ff // step):
        cut = slice(q * step, (q + 1) * step)
        up = up_v[:, cut]
        pre = nn(hidden, up)
        cdf = 0.5 * (1.0 + lax.erf(pre * ROOT_HALF))
        slope = cdf + pre * jnp.exp(-0.5 * pre * pre) * DENSITY
        act = (pre * cdf).astype(bf16)
        if q == 0:
            down_copy.wait()
        down = down_v[cut, :]
        ffn = ffn + nn(act, down)
        grad_pre = (nt(grad_low, down) * slope).astype(bf16)
        grad_hidden = grad_hidden + nt(grad_pre, up)
        grad_v[...] = tn(act, grad_low)
        split((q, slice(0, width), slice(None)), everything)
        grad_v[...] = tn(hidden, grad_pre)
        split((q, slice(width, 2 * width), slice(None)), everything)
        first = pl.ds(0, 2 * width)
        send(other_v.at[q, first, :], other_ref.at[q, first, :])
        send(own_v.at[q, first, :], own_ref.at[q, first, :])
    weighted = grad_hidden * gain
    back = scale * (weighted - normed * jnp.mean(weighted * normed, axis=-1, keepdims=True))
    grad_resid = grad_low.astype(f32) + back
    gr_v[...] = grad_resid
    send(gr_v, gr_ref)
    grad_att = grad_resid.astype(bf16)
    grad_v[...] = tn(mixed, grad_att)
    for q in range(ff // step):
        split((q, slice(2 * width, 2 * width + deep), slice(None)), slice(q * deep, (q + 1) * deep))
        last = pl.ds(2 * width, deep)
        send(other_v.at[q, last, :], other_ref.at[q, last, :])
        send(own_v.at[q, last, :], own_ref.at[q, last, :])
    out_v[...] = ((resid + ffn) * keep).astype(bf16).reshape(per, rows, width)
    send(out_v, out_ref)
    grad_mixed = nt(grad_att, ow_v[...]) * keep
    size = PER * rows
    for g in range(per // PER):

        def store(chunk, block, g=g):
            gm_v[chunk, :, g * LANES : (g + 1) * LANES] = block.astype(bf16)

        spread(grad_mixed[g * size : (g + 1) * size], store)
    send(gm_v, gm_ref)
    for copy in sent:
        copy.wait()


def value_grad_kernel(lens_ref, tok_ref, vg_ref, gain_ref, ffn_ref, vgrad_ref, joint_ref, acc_ref):
    per, rows, width = tok_ref.shape
    tok = tok_ref[...].reshape(per * rows, width).astype(f32)
    normed, _ = rms(tok)
    hidden = (normed * gain_row(gain_ref)).astype(bf16)
    vgrad = jnp.concatenate([collect(vg_ref, g) for g in range(per // PER)], axis=0)
    vgrad = (vgrad * row_keep(lens_ref, per, rows)).astype(bf16)
    vgrad_ref[...] = vgrad

    @pl.when(pl.program_id(0) == 0)
    def _():
        acc_ref[...] = jnp.zeros_like(acc_ref)

    acc_ref[...] += tn(hidden, vgrad)

    @pl.when(pl.program_id(0) == pl.num_programs(0) - 1)
    def _():
        count, tall, half = joint_ref.shape
        deep = ffn_ref.shape[1]
        rows_here = (tall - deep) // 2
        joint_ref[:, :deep, :] = ffn_ref[...]
        for n in range(count):
            for k in range(2):
                joint_ref[n, deep + k * rows_here : deep + (k + 1) * rows_here, :] = acc_ref[
                    n * rows_here : (n + 1) * rows_here, k * half : (k + 1) * half
                ].astype(bf16)


def input_grad_kernel(tok_ref, vgrad_ref, gr_ref, gain_ref, vw_ref, out_ref):
    per, rows, width = tok_ref.shape
    tok = tok_ref[...].reshape(per * rows, width).astype(f32)
    normed, scale = rms(tok)
    weighted = nt(vgrad_ref[...], vw_ref[...]) * gain_row(gain_ref)
    back = scale * (weighted - normed * jnp.mean(weighted * normed, axis=-1, keepdims=True))
    out_ref[...] = (gr_ref[...] + back).reshape(per, rows, width)


def joint_sum_kernel(joint_ref, ffn_ref, value_ref):
    total = jnp.sum(joint_ref[...].astype(f32), axis=0).astype(bf16)
    deep = ffn_ref.shape[1]
    ffn_ref[...] = jnp.broadcast_to(total[None, :deep], ffn_ref.shape)
    value_ref[...] = total[deep:]


def ring_spread_kernel(*refs):
    parts, out_ref, held = refs[:4], refs[4], refs[5]
    me = lax.axis_index("z")
    for k, part in enumerate(parts):
        held[(me - k + 4) % 4] = part[...].astype(f32)
    total = (held[0] + held[1]) + (held[2] + held[3])
    out_ref[...] = jnp.broadcast_to(total[None], out_ref.shape).astype(bf16)


def row_total(product):
    folded = sum(
        product[:, n * LANES : (n + 1) * LANES] for n in range(product.shape[1] // LANES)
    )
    return jnp.sum(folded.T, axis=0, keepdims=True)


def fold_kernel(own_ref, got_ref, *outs):
    _, _, z, _ = places()
    for k, out in enumerate(outs):
        n = (z + k) % 4
        out[...] = (own_ref[n].astype(f32) + got_ref[n].astype(f32)).astype(bf16)


def sum_kernel(*refs):
    parts, out_ref = refs[:-1], refs[-1]
    out_ref[...] = sum(part[...].astype(f32) for part in parts).astype(bf16)


def split_sum_kernel(*refs):
    parts, (own_ref, other_ref) = refs[:4], refs[4:]
    total = sum(part[...].astype(f32) for part in parts).astype(bf16)
    odd = places()[0] % 2 == 1
    own_ref[...] = jnp.where(odd, total[1], total[0])
    other_ref[...] = jnp.where(odd, total[0], total[1])


def logits_grad_kernel(part_ref, logits_ref, out_ref):
    logits = logits_ref[0].astype(f32)
    exact = jnp.exp(logits - jnp.max(logits, axis=-1, keepdims=True))
    out_ref[0] = part_ref[...].astype(f32) * exact


def finish_ffn_kernel(*refs):
    pieces, (up_ref, gain_ref), (down_out, up_out, ow_out, gain_out) = refs[:8], refs[8:10], refs[10:14]
    landed, wide, up, sems, out_sems = refs[14:]
    width = up.shape[0]
    half = landed.shape[2]
    deep = landed.shape[1] - 2 * width
    _, _, z, c = places()
    copies = [
        pltpu.make_async_copy(piece, landed.at[n], sems.at[n]) for n, piece in enumerate(pieces)
    ]
    up_copy = pltpu.make_async_copy(up_ref, up, sems.at[8])
    copies[0].start()
    up_copy.start()
    for copy in copies[1:]:
        copy.start()
    product = jnp.zeros((width, half), f32)
    out_copies = []
    for n, copy in enumerate(copies):
        copy.wait()
        ring = (z - n % 4 + 4) % 4
        side = c if n < 4 else 1 - c
        wide[n] = landed[n].astype(f32)
        lanes = pl.ds(pl.multiple_of(side * half, half), half)
        columns = pl.ds(pl.multiple_of((2 * ring + side) * half, half), half)
        targets = (
            (0, width, down_out.at[pl.ds(pl.multiple_of(ring * width, width), width), lanes]),
            (width, width, up_out.at[:, columns]),
            (2 * width, deep, ow_out.at[pl.ds(pl.multiple_of(ring * deep, deep), deep), lanes]),
        )
        for k, (first, tall, target) in enumerate(targets):
            out_copy = pltpu.make_async_copy(
                wide.at[n, pl.ds(first, tall), :], target, out_sems.at[n, k]
            )
            out_copy.start()
            out_copies.append(out_copy)
        if n == 0:
            up_copy.wait()
        product = product + up[:, columns].astype(f32) * wide[n, width : 2 * width, :]
    gain_out[...] = row_total(product) / gain_row(gain_ref)
    for out_copy in out_copies:
        out_copy.wait()


def finish_value_kernel(in_ref, vw_ref, gain_ref, out_ref, gain_out):
    count, tall, half = in_ref.shape
    rows_here = tall // 2
    for n in range(count):
        for k in range(2):
            out_ref[n * rows_here : (n + 1) * rows_here, k * half : (k + 1) * half] = in_ref[
                n, k * rows_here : (k + 1) * rows_here
            ].astype(f32)
    gain_out[...] = row_total(vw_ref[...].astype(f32) * out_ref[...]) / gain_row(gain_ref)


def params():
    return pltpu.CompilerParams(vmem_limit_bytes=63 * 1024 * 1024)


def cost(flops, size):
    return pl.CostEstimate(flops=int(flops), bytes_accessed=int(size), transcendentals=0)


def whole(*shape):
    return pl.BlockSpec(shape, lambda *_: (0,) * len(shape))


def once(*shape):
    return pl.BlockSpec(shape, lambda *_: (0,) * len(shape), pipeline_mode=pl.Buffered(1))


def shaped(dtype, *shape):
    return pltpu.HBM(shape, dtype)


def stay(*arrays):
    return [pltpu.with_memory_space_constraint(array, pltpu.HBM) for array in arrays]


def flat(x, y, z, c):
    return ((x % 4) * 4 + y % 4) * 8 + (z % 4) * 2 + c % 2


def devices():
    for i in range(128):
        s, h = divmod(i, 8)
        yield i, s // 4, s % 4, h // 2, h % 2


def shift(array, axis, step):
    return lax.ppermute(array, axis, [(i, (i + step) % 4) for i in range(4)])


def flip(array):
    return lax.ppermute(array, "core", [(0, 1), (1, 0)])


def flip_x(array):
    return lax.ppermute(array, "x", [(i, i ^ 1) for i in range(4)])


def to_plane(array, back=False):
    pairs = [(i, flat(2 * e + (a & 1), d, b, a >> 1)) for i, a, b, d, e in devices()]
    if back:
        pairs = [(j, i) for i, j in pairs]
    return lax.ppermute(array, ALL, pairs)


def around(parts, axis):
    return [parts[0]] + [shift(parts[step], axis, step) for step in (1, 2, 3)]


def swap(array, axes):
    return lax.all_to_all(array, axes, 0, 0, tiled=True)


def swap_seq(array):
    return swap(array, PLANE)


def after(array, *others):
    return lax.optimization_barrier((array,) + others)[0]


def ordered(arrays, *others):
    return list(lax.optimization_barrier((*arrays, *others)))[: len(arrays)]


def shards(
    tokens,
    lengths,
    norm_gain,
    value_weight,
    synth_logits,
    out_weight,
    ffn_gain,
    up_weight,
    down_weight,
    cotangent,
):
    group, rows, width = tokens.shape
    span = synth_logits.shape[2]
    ff = up_weight.shape[1]
    blocks = span // rows
    total_rows = group * rows
    steps = group // PER
    tile = PER * rows

    def tok_spec(n):
        return pl.BlockSpec((n, rows, width), lambda m, *_: (m, 0, 0))

    def move_spec(n):
        return pl.BlockSpec((blocks, rows, n // PER * LANES), lambda m, *_: (0, 0, m))

    def row_spec(n, columns):
        return pl.BlockSpec((n, columns), lambda m, *_: (m, 0))

    def call(kernel, grid, ins, outs, shapes, flops, size, scratch=(), prefetch=0, long=False):
        return pl.pallas_call(
            kernel,
            grid_spec=pltpu.PrefetchScalarGridSpec(
                num_scalar_prefetch=prefetch,
                grid=grid,
                in_specs=ins,
                out_specs=outs,
                scratch_shapes=scratch,
            ),
            out_shape=shapes,
            compiler_params=params(),
            cost_estimate=cost(1e13, 1e6) if long else cost(1e6, 1e5),
        )

    with jax.named_scope("logits"):
        block = synth_logits.reshape(rows, span)
        block = to_plane(block)

    with jax.named_scope("values"):
        sent_values = call(
            values_kernel,
            (steps // 2,),
            [tok_spec(2 * PER), whole(width), whole(width, width)],
            move_spec(2 * PER),
            shaped(bf16, blocks, rows, width),
            2 * total_rows * width * width,
            3e6,
            prefetch=1,
        )(lengths, *stay(tokens, norm_gain, value_weight))
        block = ordered([block], sent_values)[0]

    with jax.named_scope("logits"):
        other = flip_x(block)
        pair = jnp.concatenate([block, other])
        held = swap_seq(ordered([sent_values], other)[0]).reshape(span, width)
        pieces = [pair] + [shift(pair, "z", step) for step in (1, 2, 3)]
        pieces = pieces + [flip(piece) for piece in pieces]

    quarter = span // 4
    anywhere = pl.BlockSpec(memory_space=pl.ANY)
    with jax.named_scope("mix"):
        expo, inverse, mixed_held = call(
            mix_kernel,
            (1,),
            [anywhere] * 9,
            [anywhere] * 3,
            [shaped(bf16, span, span), shaped(f32, span, width), shaped(bf16, span, width)],
            4 * span * span * width,
            8e6,
            scratch=[
                pltpu.VMEM((8, 2 * rows, span), bf16),
                pltpu.VMEM((span, width), bf16),
                pltpu.VMEM((span, width), bf16),
                pltpu.VMEM((8, 2 * rows, span), bf16),
                pltpu.VMEM((8, 2 * rows, width), f32),
                pltpu.VMEM((8, 2 * rows, width), bf16),
                pltpu.SemaphoreType.DMA((9,)),
                pltpu.SemaphoreType.DMA((8, 3, 2)),
            ],
            prefetch=1,
        )(lengths, *pieces, held)
        got_mixed = swap_seq(mixed_held.reshape(blocks, rows, width))

    tall = ff // 4 + width + width // 4
    half_width = width // 2
    grads_shape = (4, tall, half_width)
    with jax.named_scope("ffn"):
        output, grad_resid, sent_grad, own_part, other_part = call(
            ffn_kernel,
            (1,),
            [anywhere] * 4 + [whole(width)] + [anywhere] * 2,
            [anywhere] * 5,
            [
                shaped(bf16, group, rows, width),
                shaped(f32, total_rows, width),
                shaped(bf16, blocks, rows, width),
                shaped(bf16, *grads_shape),
                shaped(bf16, *grads_shape),
            ],
            2 * total_rows * width * (6 * ff + 3 * width),
            2e7,
            scratch=[
                pltpu.VMEM((group, rows, width), bf16),
                pltpu.VMEM((group, rows, width), bf16),
                pltpu.VMEM((blocks, rows, width), bf16),
                pltpu.VMEM((width, width), bf16),
                pltpu.VMEM((width, ff), bf16),
                pltpu.VMEM((ff, width), bf16),
                pltpu.VMEM((group, rows, width), bf16),
                pltpu.VMEM((total_rows, width), f32),
                pltpu.VMEM((blocks, rows, width), bf16),
                pltpu.VMEM(grads_shape, bf16),
                pltpu.VMEM(grads_shape, bf16),
                pltpu.VMEM((width, width), f32),
                pltpu.SemaphoreType.DMA((6,)),
                pltpu.SemaphoreType.DMA((4 * ff // width + 3,)),
            ],
            prefetch=1,
        )(
            lengths,
            *stay(tokens, cotangent), got_mixed, *stay(out_weight, ffn_gain, up_weight, down_weight),
        )
        got_grad = swap_seq(sent_grad).reshape(span, width)

    def fold(own, got):
        shape = own.shape[1:]
        return call(
            fold_kernel,
            (1,),
            [whole(4, *shape)] * 2,
            [whole(*shape)] * 4,
            [shaped(bf16, *shape)] * 4,
            1e6,
            6 * math.prod(own.shape),
        )(*stay(own), got)

    with jax.named_scope("ffn_sum"):
        folded = fold(own_part, flip(other_part))
        ring_parts = around(folded, "z")
        got_grad = ordered([got_grad], folded[0])[0]

    with jax.named_scope("unmix"):
        held_grad, g_scaled, r_scaled = call(
            unmix_kernel,
            (2,),
            [pl.BlockSpec((span, 2 * quarter), lambda j: (0, j))] + [once(span, width)] * 3,
            [row_spec(2 * quarter, width), whole(span, width), whole(span, width)],
            [shaped(bf16, span, width)] * 3,
            2 * span * span * width,
            9e6,
        )(*stay(expo), got_grad, *stay(inverse, mixed_held))
        got_values = swap_seq(held_grad.reshape(blocks, rows, width))


    with jax.named_scope("scores"):
        score_shape = (4, 2, rows, span)
        own_scores, other_scores = call(
            scores_kernel,
            (2,),
            [row_spec(2 * quarter, width), row_spec(2 * quarter, width), whole(span, width)],
            [whole(*score_shape)] * 2,
            [shaped(bf16, *score_shape)] * 2,
            4 * span * span * width,
            8e6,
            scratch=[pltpu.VMEM((span, width), bf16)],
            prefetch=1,
        )(lengths, *stay(g_scaled, r_scaled), ordered([held], held_grad)[0])
        got_scores = flip(other_scores)

    with jax.named_scope("ffn_sum"):
        part = row_spec(tall // 2, half_width)
        ring_parts = ordered(ring_parts, own_scores)
        ffn_sum = call(
            sum_kernel,
            (2,),
            [part] * 4,
            part,
            shaped(bf16, tall, half_width),
            1e6,
            3e6,
            long=True,
        )(*ring_parts)

    with jax.named_scope("score_sum"):
        score_parts = fold(*ordered([own_scores, got_scores], ffn_sum))
        score_ring = around(score_parts, "z")
        got_values = ordered([got_values], score_parts[0])[0]

    with jax.named_scope("ffn_sum"):
        piece = tall // blocks
        ffn_sum = ffn_sum.reshape(blocks, piece, half_width)
        joint = piece + 2 * (width // blocks)

    with jax.named_scope("value_grad"):
        value_grad, joint_part = call(
            value_grad_kernel,
            (steps // 2,),
            [tok_spec(2 * PER), move_spec(2 * PER), whole(width), whole(blocks, piece, half_width)],
            [row_spec(2 * tile, width), whole(blocks, joint, half_width)],
            [shaped(bf16, total_rows, width), shaped(bf16, blocks, joint, half_width)],
            2 * total_rows * width * width,
            4e6,
            scratch=[pltpu.VMEM((width, width), f32)],
            prefetch=1,
        )(lengths, *stay(tokens), got_values, *stay(norm_gain), ffn_sum)
        got_joint = swap_seq(joint_part)

    with jax.named_scope("score_sum"):
        own_scores, other_scores = call(
            split_sum_kernel,
            (1,),
            [whole(2, rows, span)] * 4,
            [whole(rows, span)] * 2,
            [shaped(bf16, rows, span)] * 2,
            1e6,
            2e6,
            long=True,
        )(*ordered(score_ring, joint_part))
        got_scores = flip_x(other_scores)

    with jax.named_scope("input_grad"):
        input_grad = call(
            input_grad_kernel,
            (steps // 2,),
            [
                tok_spec(2 * PER),
                row_spec(2 * tile, width),
                row_spec(2 * tile, width),
                whole(width),
                whole(width, width),
            ],
            tok_spec(2 * PER),
            shaped(f32, group, rows, width),
            2 * total_rows * width * width,
            7e6,
        )(*stay(tokens), value_grad, *stay(*ordered([grad_resid], own_scores), norm_gain, value_weight))

    with jax.named_scope("score_sum"):
        score_total = call(
            sum_kernel,
            (1,),
            [whole(rows, span)] * 2,
            whole(rows, span),
            shaped(bf16, rows, span),
            1e6,
            1e6,
        )(*ordered([own_scores, got_scores], input_grad))
        score_back = to_plane(score_total, back=True)

    with jax.named_scope("joint_sum"):
        few = (joint - piece, half_width)
        ffn_spread, small = call(
            joint_sum_kernel,
            (1,),
            [whole(blocks, joint, half_width)],
            [whole(blocks, piece, half_width), whole(*few)],
            [shaped(bf16, blocks, piece, half_width), shaped(bf16, *few)],
            1e6,
            2e6,
        )(*ordered([got_joint], score_total))

    with jax.named_scope("value_sum"):
        small = call(
            sum_kernel,
            (1,),
            [whole(*few)] * 2,
            whole(*few),
            shaped(bf16, *few),
            1e6,
            1e6,
        )(small, flip(small))
        value_spread = call(
            ring_spread_kernel,
            (1,),
            [whole(*few)] * 4,
            whole(blocks, *few),
            shaped(bf16, blocks, *few),
            1e6,
            1e6,
            scratch=[pltpu.VMEM((4, *few), f32)],
        )(*around([small] * 4, "z"))

    with jax.named_scope("score_sum"):
        logits_grad = call(
            logits_grad_kernel,
            (1,),
            [whole(rows, span), whole(1, rows, span)],
            whole(1, rows, span),
            shaped(f32, 1, rows, span),
            1e6,
            1e6,
        )(*ordered([score_back], value_spread), synth_logits)

    with jax.named_scope("ffn_sum"):
        ffn_sum = ordered([swap_seq(ffn_spread)], value_spread)[0].reshape(tall, half_width)
        pieces = around([ffn_sum] * 4, "z")

    with jax.named_scope("value_sum"):
        value_sum = swap_seq(ordered([value_spread], ffn_sum)[0])

    with jax.named_scope("value_sum"):
        value_weight_grad, norm_gain_grad = call(
            finish_value_kernel,
            (1,),
            [whole(blocks, *few), whole(width, width), whole(width)],
            [whole(width, width), whole(1, width)],
            [shaped(f32, width, width), shaped(f32, 1, width)],
            4e6,
            2e6,
        )(value_sum, *stay(value_weight, norm_gain))

    with jax.named_scope("ffn_sum"):
        pieces = ordered(pieces, value_weight_grad, logits_grad)
        pieces = pieces + [flip(part) for part in pieces]
        down_grad, up_grad, out_grad, ffn_gain_grad = call(
            finish_ffn_kernel,
            (1,),
            [anywhere] * 9 + [whole(width)],
            [anywhere] * 3 + [whole(1, width)],
            [
                shaped(f32, ff, width),
                shaped(f32, width, ff),
                shaped(f32, width, width),
                shaped(f32, 1, width),
            ],
            4e6,
            13e6,
            scratch=[
                pltpu.VMEM((8, tall, half_width), bf16),
                pltpu.VMEM((8, tall, half_width), f32),
                pltpu.VMEM((width, ff), bf16),
                pltpu.SemaphoreType.DMA((9,)),
                pltpu.SemaphoreType.DMA((8, 3)),
            ],
        )(*pieces, *stay(up_weight, ffn_gain))

    return (
        output,
        input_grad,
        norm_gain_grad.reshape(width),
        value_weight_grad,
        logits_grad,
        out_grad,
        ffn_gain_grad.reshape(width),
        up_grad,
        down_grad,
    )


def solution(mesh):
    token_spec = P(("z", "core"), PLANE, None)
    placed = (
        token_spec,
        P(),
        P(),
        P(),
        token_spec,
        P(),
        P(),
        P(),
        P(),
        token_spec,
    )
    fine = jax.sharding.Mesh(mesh.devices.reshape(4, 4, 4, 2), ALL)
    return jax.shard_map(
        shards,
        mesh=fine,
        in_specs=placed,
        out_specs=(token_spec, token_spec, P(), P(), token_spec, P(), P(), P(), P()),
        check_vma=False,
    )
```

```python
import functools
import math

import jax
import jax.numpy as jnp
from jax import lax
from jax.experimental import pallas as pl
from jax.experimental.pallas import tpu as pltpu
from jax.sharding import PartitionSpec as P

EPS = 1e-06
ROOT_HALF = 1.0 / math.sqrt(2.0)
DENSITY = 1.0 / math.sqrt(2.0 * math.pi)
LANES = 128
CHUNK = 32
PER = LANES // CHUNK
PLANE = ("x", "y")
CHIPS = ("x", "y", "z")
ALL = ("x", "y", "z", "core")
bf16 = jnp.bfloat16
f32 = jnp.float32


def nt(left, right):
    return lax.dot_general(left, right, (((1,), (1,)), ((), ())), preferred_element_type=f32)


def tn(left, right):
    return lax.dot_general(left, right, (((0,), (0,)), ((), ())), preferred_element_type=f32)


def nn(left, right):
    return jnp.dot(left, right, preferred_element_type=f32)


def lane_groups(rows):
    return lax.broadcasted_iota(jnp.int32, (rows, LANES), 1) // CHUNK


def pick(groups, parts):
    out = parts[PER - 1]
    for l in range(PER - 2, -1, -1):
        out = jnp.where(groups == l, parts[l], out)
    return out


def seat(chunk):
    return chunk % 4 * 4 + chunk // 4


def spread(value, store):
    rows = value.shape[0] // PER
    groups = lane_groups(rows)
    for q in range(value.shape[1] // LANES):
        turned = []
        for r in range(PER):
            piece = value[r * rows : (r + 1) * rows, q * LANES : (q + 1) * LANES]
            turned.append(pltpu.roll(piece, CHUNK * r, 1) if r else piece)
        for k in range(PER):
            store(seat(q * PER + k), pick(groups, [turned[(l - k) % PER] for l in range(PER)]))


def collect(ref, group):
    chunks, rows, _ = ref.shape
    lanes = slice(group * LANES, (group + 1) * LANES)
    groups = lane_groups(rows)
    columns = []
    for q in range(chunks // PER):
        loaded = [ref[seat(q * PER + k), :, lanes].astype(f32) for k in range(PER)]
        parts = []
        for r in range(PER):
            mixed = pick(groups, [loaded[(l - r) % PER] for l in range(PER)])
            parts.append(pltpu.roll(mixed, LANES - CHUNK * r, 1) if r else mixed)
        columns.append(jnp.concatenate(parts, axis=0))
    return jnp.concatenate(columns, axis=1)


def places():
    return tuple(lax.axis_index(axis) for axis in ALL)


def first_bucket(lens_ref):
    _, _, z, c = places()
    return (z * 2 + c) * (lens_ref.shape[0] // 8)


def row_keep(lens_ref, buckets, rows):
    x, y, _, _ = places()
    spot = (x * 4 + y) * rows + lax.broadcasted_iota(jnp.int32, (rows, 1), 0)
    first = first_bucket(lens_ref) + pl.program_id(0) * buckets
    parts = [(spot < lens_ref[first + r]).astype(f32) for r in range(buckets)]
    return jnp.concatenate(parts, axis=0)


def gain_row(gain_ref):
    return gain_ref[...].astype(f32).reshape(1, gain_ref.shape[0])


def rms(values):
    scale = lax.rsqrt(jnp.mean(values * values, axis=-1, keepdims=True) + EPS)
    return values * scale, scale


def values_kernel(lens_ref, tok_ref, gain_ref, vw_ref, out_ref):
    per, rows, width = tok_ref.shape
    tok = tok_ref[...].reshape(per * rows, width).astype(f32)
    normed, _ = rms(tok)
    hidden = (normed * gain_row(gain_ref)).astype(bf16)
    val = nn(hidden, vw_ref[...]) * row_keep(lens_ref, per, rows)

    size = PER * rows
    for g in range(per // PER):

        def store(chunk, block, g=g):
            out_ref[chunk, :, g * LANES : (g + 1) * LANES] = block.astype(bf16)

        spread(val[g * size : (g + 1) * size], store)


def lane_lengths(lens_ref, lanes):
    x, _, _, _ = places()
    group = lanes // CHUNK
    first = first_bucket(lens_ref)
    lane = lax.broadcasted_iota(jnp.int32, (1, lanes), 1) // CHUNK
    lens = jnp.zeros((1, lanes), jnp.int32)
    for n in range(group):
        m, l = divmod(n, PER)
        lens = jnp.where(lane == n, lens_ref[first + m * PER + (l - x + PER) % PER], lens)
    return lens


def mix_kernel(lens_ref, *refs):
    count = len(refs) - 12
    pieces = refs[:count]
    held_ref, exp_out, inv_out, mix_out = refs[count : count + 4]
    landed, held, keep, expo, inverse, mixed, sems, out_sems = refs[count + 4 :]
    span, lanes = held.shape
    x, _, z, c = places()
    half = pieces[0].shape[0] // 2
    copies = [
        pltpu.make_async_copy(piece, landed.at[n], sems.at[n]) for n, piece in enumerate(pieces)
    ]
    held_copy = pltpu.make_async_copy(held_ref, held, sems.at[count])
    copies[0].start()
    held_copy.start()
    for copy in copies[1:]:
        copy.start()
    lens = lane_lengths(lens_ref, lanes)
    place = lax.broadcasted_iota(jnp.int32, (span, lanes), 0)
    keep[...] = (place < lens).astype(f32).astype(bf16)
    out_copies = []
    deep = 4 * 2 * half
    for batch in range(2):
        starts = []
        bounds = []
        for n in range(4 * batch, 4 * batch + 4):
            copies[n].wait()
            core = c if batch == 0 else 1 - c
            ring = (z - n % 4 + 4) % 4
            for k in range(2):
                start = ((core * 2 + (x + k) % 2) * 4 + ring) * half
                starts.append(pl.multiple_of(start, half))
                bounds.append(lens - start)
        cut = pl.ds(4 * batch, 4)
        logits = landed[cut].reshape(deep, span).astype(f32)
        part = jnp.exp(logits - jnp.max(logits, axis=-1, keepdims=True)).astype(bf16)
        expo[cut] = part.reshape(4, 2 * half, span)
        totals = nn(part, keep[...])
        row = lax.broadcasted_iota(jnp.int32, (half, lanes), 0)
        kept = jnp.concatenate([(row < bound).astype(f32) for bound in bounds], axis=0)
        inverted = kept / totals
        inverse[cut] = inverted.reshape(4, 2 * half, lanes)
        if batch == 0:
            held_copy.wait()
        mixed[cut] = (nn(part, held[...]) * inverted).astype(bf16).reshape(4, 2 * half, lanes)
        for n in range(4 * batch, 4 * batch + 4):
            for j, (source, target) in enumerate(
                ((mixed, mix_out), (expo, exp_out), (inverse, inv_out))
            ):
                for k in range(2):
                    copy = pltpu.make_async_copy(
                        source.at[n, pl.ds(k * half, half), :],
                        target.at[pl.ds(starts[2 * (n - 4 * batch) + k], half), :],
                        out_sems.at[n, j, k],
                    )
                    copy.start()
                    out_copies.append(copy)
    for copy in out_copies:
        copy.wait()


def unmix_kernel(exp_ref, gm_ref, inv_ref, mixed_ref, out_ref, g_ref, r_ref):
    @pl.when(pl.program_id(0) == 0)
    def _():
        scaled = gm_ref[...].astype(f32) * inv_ref[...]
        g_ref[...] = scaled.astype(bf16)
        r_ref[...] = (scaled * mixed_ref[...].astype(f32)).astype(bf16)

    out_ref[...] = tn(exp_ref[...], g_ref[...]).astype(bf16)


def scores_kernel(lens_ref, g_ref, r_ref, val_ref, own_ref, other_ref, keep_ref):
    span, lanes = val_ref.shape

    @pl.when(pl.program_id(0) == 0)
    def _():
        place = lax.broadcasted_iota(jnp.int32, (span, lanes), 0)
        keep_ref[...] = (place < lane_lengths(lens_ref, lanes)).astype(f32).astype(bf16)

    out = (nt(g_ref[...], val_ref[...]) - nt(r_ref[...], keep_ref[...])).astype(bf16)
    step = pl.program_id(0)
    _, _, _, c = places()
    rings, bits, rows, _ = own_ref.shape

    def store(ref):
        for bit in range(bits):
            for n in range(rings):
                first = (bit * rings + n) * rows
                ref[n, bit] = out[first : first + rows]

    @pl.when(step == c)
    def _():
        store(own_ref)

    @pl.when(step != c)
    def _():
        store(other_ref)


def ffn_kernel(lens_ref, *refs):
    ins, refs = refs[:7], refs[7:]
    tok_in, cot_in, mix_in, ow_in, gain_ref, up_in, down_in = ins
    out_ref, gr_ref, gm_ref, own_ref, other_ref = refs[:5]
    tok_v, cot_v, mix_v, ow_v, up_v, down_v, out_v, gr_v, gm_v, own_v, other_v, grad_v = refs[5:17]
    sems, out_sems = refs[17:]
    per, rows, width = tok_v.shape
    n = per * rows
    ff = up_v.shape[1]
    step = width
    _, _, _, core = places()
    half = width // 2
    deep = own_v.shape[1] - 2 * width

    def fetch(k, source, target):
        copy = pltpu.make_async_copy(source, target, sems.at[k])
        copy.start()
        return copy

    mix_copy = fetch(0, mix_in, mix_v)
    ow_copy = fetch(1, ow_in, ow_v)
    tok_copy = fetch(2, tok_in, tok_v)
    up_copy = fetch(3, up_in, up_v)
    cot_copy = fetch(4, cot_in, cot_v)
    down_copy = fetch(5, down_in, down_v)
    sent = []

    def send(source, target):
        copy = pltpu.make_async_copy(source, target, out_sems.at[len(sent)])
        copy.start()
        sent.append(copy)

    keep = row_keep(lens_ref, per, rows)
    mix_copy.wait()
    mixed = jnp.concatenate([collect(mix_v, g) for g in range(per // PER)], axis=0).astype(bf16)
    ow_copy.wait()
    tok_copy.wait()
    resid = tok_v[...].reshape(n, width).astype(f32) + nn(mixed, ow_v[...])
    normed, scale = rms(resid)
    gain = gain_row(gain_ref)
    hidden = (normed * gain).astype(bf16)
    cot_copy.wait()
    grad_low = (cot_v[...].reshape(n, width).astype(f32) * keep).astype(bf16)
    up_copy.wait()

    def add(ref, spot, side, source):
        lanes = pl.ds(pl.multiple_of(side * half, half), half)
        ref[spot] = grad_v[source, lanes].astype(bf16)

    def split(spot, source):
        add(other_v, spot, 1 - core, source)
        add(own_v, spot, core, source)

    ffn = jnp.zeros((n, width), f32)
    grad_hidden = jnp.zeros((n, width), f32)
    everything = slice(0, width)
    for q in range(ff // step):
        cut = slice(q * step, (q + 1) * step)
        up = up_v[:, cut]
        pre = nn(hidden, up)
        cdf = 0.5 * (1.0 + lax.erf(pre * ROOT_HALF))
        slope = cdf + pre * jnp.exp(-0.5 * pre * pre) * DENSITY
        act = (pre * cdf).astype(bf16)
        if q == 0:
            down_copy.wait()
        down = down_v[cut, :]
        ffn = ffn + nn(act, down)
        grad_pre = (nt(grad_low, down) * slope).astype(bf16)
        grad_hidden = grad_hidden + nt(grad_pre, up)
        grad_v[...] = tn(act, grad_low)
        split((q, slice(0, width), slice(None)), everything)
        grad_v[...] = tn(hidden, grad_pre)
        split((q, slice(width, 2 * width), slice(None)), everything)
        first = pl.ds(0, 2 * width)
        send(other_v.at[q, first, :], other_ref.at[q, first, :])
        send(own_v.at[q, first, :], own_ref.at[q, first, :])
    weighted = grad_hidden * gain
    back = scale * (weighted - normed * jnp.mean(weighted * normed, axis=-1, keepdims=True))
    grad_resid = grad_low.astype(f32) + back
    gr_v[...] = grad_resid
    send(gr_v, gr_ref)
    grad_att = grad_resid.astype(bf16)
    grad_v[...] = tn(mixed, grad_att)
    for q in range(ff // step):
        split((q, slice(2 * width, 2 * width + deep), slice(None)), slice(q * deep, (q + 1) * deep))
        last = pl.ds(2 * width, deep)
        send(other_v.at[q, last, :], other_ref.at[q, last, :])
        send(own_v.at[q, last, :], own_ref.at[q, last, :])
    out_v[...] = ((resid + ffn) * keep).astype(bf16).reshape(per, rows, width)
    send(out_v, out_ref)
    grad_mixed = nt(grad_att, ow_v[...]) * keep
    size = PER * rows
    for g in range(per // PER):

        def store(chunk, block, g=g):
            gm_v[chunk, :, g * LANES : (g + 1) * LANES] = block.astype(bf16)

        spread(grad_mixed[g * size : (g + 1) * size], store)
    send(gm_v, gm_ref)
    for copy in sent:
        copy.wait()


def value_grad_kernel(lens_ref, tok_ref, vg_ref, gain_ref, ffn_ref, vgrad_ref, joint_ref, acc_ref):
    per, rows, width = tok_ref.shape
    tok = tok_ref[...].reshape(per * rows, width).astype(f32)
    normed, _ = rms(tok)
    hidden = (normed * gain_row(gain_ref)).astype(bf16)
    vgrad = jnp.concatenate([collect(vg_ref, g) for g in range(per // PER)], axis=0)
    vgrad = (vgrad * row_keep(lens_ref, per, rows)).astype(bf16)
    vgrad_ref[...] = vgrad

    @pl.when(pl.program_id(0) == 0)
    def _():
        acc_ref[...] = jnp.zeros_like(acc_ref)

    acc_ref[...] += tn(hidden, vgrad)

    @pl.when(pl.program_id(0) == pl.num_programs(0) - 1)
    def _():
        count, tall, half = joint_ref.shape
        deep = ffn_ref.shape[1]
        rows_here = (tall - deep) // 2
        joint_ref[:, :deep, :] = ffn_ref[...]
        for n in range(count):
            for k in range(2):
                joint_ref[n, deep + k * rows_here : deep + (k + 1) * rows_here, :] = acc_ref[
                    n * rows_here : (n + 1) * rows_here, k * half : (k + 1) * half
                ].astype(bf16)


def input_grad_kernel(tok_ref, vgrad_ref, gr_ref, gain_ref, vw_ref, out_ref):
    per, rows, width = tok_ref.shape
    tok = tok_ref[...].reshape(per * rows, width).astype(f32)
    normed, scale = rms(tok)
    weighted = nt(vgrad_ref[...], vw_ref[...]) * gain_row(gain_ref)
    back = scale * (weighted - normed * jnp.mean(weighted * normed, axis=-1, keepdims=True))
    out_ref[...] = (gr_ref[...] + back).reshape(per, rows, width)


def joint_sum_kernel(joint_ref, ffn_ref, value_ref):
    total = jnp.sum(joint_ref[...].astype(f32), axis=0).astype(bf16)
    deep = ffn_ref.shape[1]
    ffn_ref[...] = jnp.broadcast_to(total[None, :deep], ffn_ref.shape)
    value_ref[...] = total[deep:]


def ring_spread_kernel(*refs):
    parts, out_ref, held = refs[:4], refs[4], refs[5]
    me = lax.axis_index("z")
    for k, part in enumerate(parts):
        held[(me - k + 4) % 4] = part[...].astype(f32)
    total = (held[0] + held[1]) + (held[2] + held[3])
    out_ref[...] = jnp.broadcast_to(total[None], out_ref.shape).astype(bf16)


def row_total(product):
    folded = sum(
        product[:, n * LANES : (n + 1) * LANES] for n in range(product.shape[1] // LANES)
    )
    return jnp.sum(folded.T, axis=0, keepdims=True)


def fold_kernel(own_ref, got_ref, *outs):
    _, _, z, _ = places()
    for k, out in enumerate(outs):
        n = (z + k) % 4
        out[...] = (own_ref[n].astype(f32) + got_ref[n].astype(f32)).astype(bf16)


def sum_kernel(*refs):
    parts, out_ref = refs[:-1], refs[-1]
    out_ref[...] = sum(part[...].astype(f32) for part in parts).astype(bf16)


def split_sum_kernel(*refs):
    parts, (own_ref, other_ref) = refs[:4], refs[4:]
    total = sum(part[...].astype(f32) for part in parts).astype(bf16)
    odd = places()[0] % 2 == 1
    own_ref[...] = jnp.where(odd, total[1], total[0])
    other_ref[...] = jnp.where(odd, total[0], total[1])


def logits_grad_kernel(part_ref, logits_ref, out_ref):
    logits = logits_ref[0].astype(f32)
    exact = jnp.exp(logits - jnp.max(logits, axis=-1, keepdims=True))
    out_ref[0] = part_ref[...].astype(f32) * exact


def finish_ffn_kernel(*refs):
    pieces, (up_ref, gain_ref), (down_out, up_out, ow_out, gain_out) = refs[:8], refs[8:10], refs[10:14]
    landed, wide, up, sems, out_sems = refs[14:]
    width = up.shape[0]
    half = landed.shape[2]
    deep = landed.shape[1] - 2 * width
    _, _, z, c = places()
    copies = [
        pltpu.make_async_copy(piece, landed.at[n], sems.at[n]) for n, piece in enumerate(pieces)
    ]
    up_copy = pltpu.make_async_copy(up_ref, up, sems.at[8])
    copies[0].start()
    up_copy.start()
    for copy in copies[1:]:
        copy.start()
    product = jnp.zeros((width, half), f32)
    out_copies = []
    for n, copy in enumerate(copies):
        copy.wait()
        ring = (z - n % 4 + 4) % 4
        side = c if n < 4 else 1 - c
        wide[n] = landed[n].astype(f32)
        lanes = pl.ds(pl.multiple_of(side * half, half), half)
        columns = pl.ds(pl.multiple_of((2 * ring + side) * half, half), half)
        targets = (
            (0, width, down_out.at[pl.ds(pl.multiple_of(ring * width, width), width), lanes]),
            (width, width, up_out.at[:, columns]),
            (2 * width, deep, ow_out.at[pl.ds(pl.multiple_of(ring * deep, deep), deep), lanes]),
        )
        for k, (first, tall, target) in enumerate(targets):
            out_copy = pltpu.make_async_copy(
                wide.at[n, pl.ds(first, tall), :], target, out_sems.at[n, k]
            )
            out_copy.start()
            out_copies.append(out_copy)
        if n == 0:
            up_copy.wait()
        product = product + up[:, columns].astype(f32) * wide[n, width : 2 * width, :]
    gain_out[...] = row_total(product) / gain_row(gain_ref)
    for out_copy in out_copies:
        out_copy.wait()


def finish_value_kernel(in_ref, vw_ref, gain_ref, out_ref, gain_out):
    count, tall, half = in_ref.shape
    rows_here = tall // 2
    for n in range(count):
        for k in range(2):
            out_ref[n * rows_here : (n + 1) * rows_here, k * half : (k + 1) * half] = in_ref[
                n, k * rows_here : (k + 1) * rows_here
            ].astype(f32)
    gain_out[...] = row_total(vw_ref[...].astype(f32) * out_ref[...]) / gain_row(gain_ref)


def params(mib):
    return pltpu.CompilerParams(vmem_limit_bytes=mib * 1024 * 1024)


def cost(flops, size):
    return pl.CostEstimate(flops=int(flops), bytes_accessed=int(size), transcendentals=0)


def whole(*shape):
    return pl.BlockSpec(shape, lambda *_: (0,) * len(shape))


def once(*shape):
    return pl.BlockSpec(shape, lambda *_: (0,) * len(shape), pipeline_mode=pl.Buffered(1))


def shaped(dtype, *shape):
    return pltpu.HBM(shape, dtype)


def stay(*arrays):
    return [pltpu.with_memory_space_constraint(array, pltpu.HBM) for array in arrays]


def flat(x, y, z, c):
    return ((x % 4) * 4 + y % 4) * 8 + (z % 4) * 2 + c % 2


def devices():
    for i in range(128):
        s, h = divmod(i, 8)
        yield i, s // 4, s % 4, h // 2, h % 2


def shift(array, axis, step):
    return lax.ppermute(array, axis, [(i, (i + step) % 4) for i in range(4)])


def flip(array):
    return lax.ppermute(array, "core", [(0, 1), (1, 0)])


def flip_x(array):
    return lax.ppermute(array, "x", [(i, i ^ 1) for i in range(4)])


def to_plane(array, back=False):
    pairs = [(i, flat(2 * e + (a & 1), d, b, a >> 1)) for i, a, b, d, e in devices()]
    if back:
        pairs = [(j, i) for i, j in pairs]
    return lax.ppermute(array, ALL, pairs)


def around(parts, axis):
    return [parts[0]] + [shift(parts[step], axis, step) for step in (1, 2, 3)]


def swap(array, axes):
    return lax.all_to_all(array, axes, 0, 0, tiled=True)


def swap_seq(array):
    return swap(array, PLANE)


def after(array, *others):
    return lax.optimization_barrier((array,) + others)[0]


def ordered(arrays, *others):
    return list(lax.optimization_barrier((*arrays, *others)))[: len(arrays)]


def shards(
    tokens,
    lengths,
    norm_gain,
    value_weight,
    synth_logits,
    out_weight,
    ffn_gain,
    up_weight,
    down_weight,
    cotangent,
):
    group, rows, width = tokens.shape
    span = synth_logits.shape[2]
    ff = up_weight.shape[1]
    blocks = span // rows
    total_rows = group * rows
    steps = group // PER
    tile = PER * rows

    def tok_spec(n):
        return pl.BlockSpec((n, rows, width), lambda m, *_: (m, 0, 0))

    def move_spec(n):
        return pl.BlockSpec((blocks, rows, n // PER * LANES), lambda m, *_: (0, 0, m))

    def row_spec(n, columns):
        return pl.BlockSpec((n, columns), lambda m, *_: (m, 0))

    def call(kernel, grid, ins, outs, shapes, flops, size, scratch=(), prefetch=0, long=False, mib=40):
        return pl.pallas_call(
            kernel,
            grid_spec=pltpu.PrefetchScalarGridSpec(
                num_scalar_prefetch=prefetch,
                grid=grid,
                in_specs=ins,
                out_specs=outs,
                scratch_shapes=scratch,
            ),
            out_shape=shapes,
            compiler_params=params(mib),
            cost_estimate=cost(1e13, 1e6) if long else cost(1e6, 1e5),
        )

    with jax.named_scope("logits"):
        block = synth_logits.reshape(rows, span)
        block = to_plane(block)

    with jax.named_scope("values"):
        sent_values = call(
            values_kernel,
            (steps // 2,),
            [tok_spec(2 * PER), whole(width), whole(width, width)],
            move_spec(2 * PER),
            shaped(bf16, blocks, rows, width),
            2 * total_rows * width * width,
            3e6,
            prefetch=1,
        )(lengths, *stay(tokens, norm_gain, value_weight))
        block = ordered([block], sent_values)[0]

    with jax.named_scope("logits"):
        other = flip_x(block)
        pair = jnp.concatenate([block, other])
        held = swap_seq(ordered([sent_values], other)[0]).reshape(span, width)
        pieces = [pair] + [shift(pair, "z", step) for step in (1, 2, 3)]
        pieces = pieces + [flip(piece) for piece in pieces]

    quarter = span // 4
    anywhere = pl.BlockSpec(memory_space=pl.ANY)
    with jax.named_scope("mix"):
        expo, inverse, mixed_held = call(
            mix_kernel,
            (1,),
            [anywhere] * 9,
            [anywhere] * 3,
            [shaped(bf16, span, span), shaped(f32, span, width), shaped(bf16, span, width)],
            4 * span * span * width,
            8e6,
            scratch=[
                pltpu.VMEM((8, 2 * rows, span), bf16),
                pltpu.VMEM((span, width), bf16),
                pltpu.VMEM((span, width), bf16),
                pltpu.VMEM((8, 2 * rows, span), bf16),
                pltpu.VMEM((8, 2 * rows, width), f32),
                pltpu.VMEM((8, 2 * rows, width), bf16),
                pltpu.SemaphoreType.DMA((9,)),
                pltpu.SemaphoreType.DMA((8, 3, 2)),
            ],
            prefetch=1,
        )(lengths, *pieces, held)
        got_mixed = swap_seq(mixed_held.reshape(blocks, rows, width))

    tall = ff // 4 + width + width // 4
    half_width = width // 2
    grads_shape = (4, tall, half_width)
    with jax.named_scope("ffn"):
        output, grad_resid, sent_grad, own_part, other_part = call(
            ffn_kernel,
            (1,),
            [anywhere] * 4 + [whole(width)] + [anywhere] * 2,
            [anywhere] * 5,
            [
                shaped(bf16, group, rows, width),
                shaped(f32, total_rows, width),
                shaped(bf16, blocks, rows, width),
                shaped(bf16, *grads_shape),
                shaped(bf16, *grads_shape),
            ],
            2 * total_rows * width * (6 * ff + 3 * width),
            2e7,
            scratch=[
                pltpu.VMEM((group, rows, width), bf16),
                pltpu.VMEM((group, rows, width), bf16),
                pltpu.VMEM((blocks, rows, width), bf16),
                pltpu.VMEM((width, width), bf16),
                pltpu.VMEM((width, ff), bf16),
                pltpu.VMEM((ff, width), bf16),
                pltpu.VMEM((group, rows, width), bf16),
                pltpu.VMEM((total_rows, width), f32),
                pltpu.VMEM((blocks, rows, width), bf16),
                pltpu.VMEM(grads_shape, bf16),
                pltpu.VMEM(grads_shape, bf16),
                pltpu.VMEM((width, width), f32),
                pltpu.SemaphoreType.DMA((6,)),
                pltpu.SemaphoreType.DMA((4 * ff // width + 3,)),
            ],
            prefetch=1,
            mib=54,
        )(
            lengths,
            *stay(tokens, cotangent), got_mixed, *stay(out_weight, ffn_gain, up_weight, down_weight),
        )
        got_grad = swap_seq(sent_grad).reshape(span, width)

    def fold(own, got):
        shape = own.shape[1:]
        return call(
            fold_kernel,
            (1,),
            [whole(4, *shape)] * 2,
            [whole(*shape)] * 4,
            [shaped(bf16, *shape)] * 4,
            1e6,
            6 * math.prod(own.shape),
        )(*stay(own), got)

    with jax.named_scope("ffn_sum"):
        folded = fold(own_part, flip(other_part))
        ring_parts = around(folded, "z")
        got_grad = ordered([got_grad], folded[0])[0]

    with jax.named_scope("unmix"):
        held_grad, g_scaled, r_scaled = call(
            unmix_kernel,
            (2,),
            [pl.BlockSpec((span, 2 * quarter), lambda j: (0, j))] + [once(span, width)] * 3,
            [row_spec(2 * quarter, width), whole(span, width), whole(span, width)],
            [shaped(bf16, span, width)] * 3,
            2 * span * span * width,
            9e6,
        )(*stay(expo), got_grad, *stay(inverse, mixed_held))
        got_values = swap_seq(held_grad.reshape(blocks, rows, width))


    with jax.named_scope("scores"):
        score_shape = (4, 2, rows, span)
        own_scores, other_scores = call(
            scores_kernel,
            (2,),
            [row_spec(2 * quarter, width), row_spec(2 * quarter, width), whole(span, width)],
            [whole(*score_shape)] * 2,
            [shaped(bf16, *score_shape)] * 2,
            4 * span * span * width,
            8e6,
            scratch=[pltpu.VMEM((span, width), bf16)],
            prefetch=1,
        )(lengths, *stay(g_scaled, r_scaled), ordered([held], held_grad)[0])
        got_scores = flip(other_scores)

    with jax.named_scope("ffn_sum"):
        part = row_spec(tall // 2, half_width)
        ring_parts = ordered(ring_parts, own_scores)
        ffn_sum = call(
            sum_kernel,
            (2,),
            [part] * 4,
            part,
            shaped(bf16, tall, half_width),
            1e6,
            3e6,
            long=True,
        )(*ring_parts)

    with jax.named_scope("score_sum"):
        score_parts = fold(*ordered([own_scores, got_scores], ffn_sum))
        score_ring = around(score_parts, "z")
        got_values = ordered([got_values], score_parts[0])[0]

    with jax.named_scope("ffn_sum"):
        piece = tall // blocks
        ffn_sum = ffn_sum.reshape(blocks, piece, half_width)
        joint = piece + 2 * (width // blocks)

    with jax.named_scope("value_grad"):
        value_grad, joint_part = call(
            value_grad_kernel,
            (steps // 2,),
            [tok_spec(2 * PER), move_spec(2 * PER), whole(width), whole(blocks, piece, half_width)],
            [row_spec(2 * tile, width), whole(blocks, joint, half_width)],
            [shaped(bf16, total_rows, width), shaped(bf16, blocks, joint, half_width)],
            2 * total_rows * width * width,
            4e6,
            scratch=[pltpu.VMEM((width, width), f32)],
            prefetch=1,
        )(lengths, *stay(tokens), got_values, *stay(norm_gain), ffn_sum)
        got_joint = swap_seq(joint_part)

    with jax.named_scope("score_sum"):
        own_scores, other_scores = call(
            split_sum_kernel,
            (1,),
            [whole(2, rows, span)] * 4,
            [whole(rows, span)] * 2,
            [shaped(bf16, rows, span)] * 2,
            1e6,
            2e6,
            long=True,
        )(*ordered(score_ring, joint_part))
        got_scores = flip_x(other_scores)

    with jax.named_scope("input_grad"):
        input_grad = call(
            input_grad_kernel,
            (steps // 2,),
            [
                tok_spec(2 * PER),
                row_spec(2 * tile, width),
                row_spec(2 * tile, width),
                whole(width),
                whole(width, width),
            ],
            tok_spec(2 * PER),
            shaped(f32, group, rows, width),
            2 * total_rows * width * width,
            7e6,
        )(*stay(tokens), value_grad, *stay(*ordered([grad_resid], own_scores), norm_gain, value_weight))

    with jax.named_scope("score_sum"):
        score_total = call(
            sum_kernel,
            (1,),
            [whole(rows, span)] * 2,
            whole(rows, span),
            shaped(bf16, rows, span),
            1e6,
            1e6,
        )(*ordered([own_scores, got_scores], input_grad))
        score_back = to_plane(score_total, back=True)

    with jax.named_scope("joint_sum"):
        few = (joint - piece, half_width)
        ffn_spread, small = call(
            joint_sum_kernel,
            (1,),
            [whole(blocks, joint, half_width)],
            [whole(blocks, piece, half_width), whole(*few)],
            [shaped(bf16, blocks, piece, half_width), shaped(bf16, *few)],
            1e6,
            2e6,
        )(*ordered([got_joint], score_total))

    with jax.named_scope("value_sum"):
        small = call(
            sum_kernel,
            (1,),
            [whole(*few)] * 2,
            whole(*few),
            shaped(bf16, *few),
            1e6,
            1e6,
        )(small, flip(small))
        value_spread = call(
            ring_spread_kernel,
            (1,),
            [whole(*few)] * 4,
            whole(blocks, *few),
            shaped(bf16, blocks, *few),
            1e6,
            1e6,
            scratch=[pltpu.VMEM((4, *few), f32)],
        )(*around([small] * 4, "z"))

    with jax.named_scope("score_sum"):
        logits_grad = call(
            logits_grad_kernel,
            (1,),
            [whole(rows, span), whole(1, rows, span)],
            whole(1, rows, span),
            shaped(f32, 1, rows, span),
            1e6,
            1e6,
        )(*ordered([score_back], value_spread), synth_logits)

    with jax.named_scope("ffn_sum"):
        ffn_sum = ordered([swap_seq(ffn_spread)], value_spread)[0].reshape(tall, half_width)
        pieces = around([ffn_sum] * 4, "z")

    with jax.named_scope("value_sum"):
        value_sum = swap_seq(ordered([value_spread], ffn_sum)[0])

    with jax.named_scope("value_sum"):
        value_weight_grad, norm_gain_grad = call(
            finish_value_kernel,
            (1,),
            [whole(blocks, *few), whole(width, width), whole(width)],
            [whole(width, width), whole(1, width)],
            [shaped(f32, width, width), shaped(f32, 1, width)],
            4e6,
            2e6,
        )(value_sum, *stay(value_weight, norm_gain))

    with jax.named_scope("ffn_sum"):
        pieces = ordered(pieces, value_weight_grad, logits_grad)
        pieces = pieces + [flip(part) for part in pieces]
        down_grad, up_grad, out_grad, ffn_gain_grad = call(
            finish_ffn_kernel,
            (1,),
            [anywhere] * 9 + [whole(width)],
            [anywhere] * 3 + [whole(1, width)],
            [
                shaped(f32, ff, width),
                shaped(f32, width, ff),
                shaped(f32, width, width),
                shaped(f32, 1, width),
            ],
            4e6,
            13e6,
            scratch=[
                pltpu.VMEM((8, tall, half_width), bf16),
                pltpu.VMEM((8, tall, half_width), f32),
                pltpu.VMEM((width, ff), bf16),
                pltpu.SemaphoreType.DMA((9,)),
                pltpu.SemaphoreType.DMA((8, 3)),
            ],
        )(*pieces, *stay(up_weight, ffn_gain))

    return (
        output,
        input_grad,
        norm_gain_grad.reshape(width),
        value_weight_grad,
        logits_grad,
        out_grad,
        ffn_gain_grad.reshape(width),
        up_grad,
        down_grad,
    )


def solution(mesh):
    token_spec = P(("z", "core"), PLANE, None)
    placed = (
        token_spec,
        P(),
        P(),
        P(),
        token_spec,
        P(),
        P(),
        P(),
        P(),
        token_spec,
    )
    fine = jax.sharding.Mesh(mesh.devices.reshape(4, 4, 4, 2), ALL)
    return jax.shard_map(
        shards,
        mesh=fine,
        in_specs=placed,
        out_specs=(token_spec, token_spec, P(), P(), token_spec, P(), P(), P(), P()),
        check_vma=False,
    )
```

```python
import functools
import math

import jax
import jax.numpy as jnp
from jax import lax
from jax.experimental import pallas as pl
from jax.experimental.pallas import tpu as pltpu
from jax.sharding import PartitionSpec as P

EPS = 1e-06
ROOT_HALF = 1.0 / math.sqrt(2.0)
DENSITY = 1.0 / math.sqrt(2.0 * math.pi)
LANES = 128
CHUNK = 32
PER = LANES // CHUNK
PLANE = ("x", "y")
CHIPS = ("x", "y", "z")
ALL = ("x", "y", "z", "core")
bf16 = jnp.bfloat16
f32 = jnp.float32


def nt(left, right):
    return lax.dot_general(left, right, (((1,), (1,)), ((), ())), preferred_element_type=f32)


def tn(left, right):
    return lax.dot_general(left, right, (((0,), (0,)), ((), ())), preferred_element_type=f32)


def nn(left, right):
    return jnp.dot(left, right, preferred_element_type=f32)


def lane_groups(rows):
    return lax.broadcasted_iota(jnp.int32, (rows, LANES), 1) // CHUNK


def pick(groups, parts):
    out = parts[PER - 1]
    for l in range(PER - 2, -1, -1):
        out = jnp.where(groups == l, parts[l], out)
    return out


def seat(chunk):
    return chunk % 4 * 4 + chunk // 4


def spread(value, store):
    rows = value.shape[0] // PER
    groups = lane_groups(rows)
    for q in range(value.shape[1] // LANES):
        turned = []
        for r in range(PER):
            piece = value[r * rows : (r + 1) * rows, q * LANES : (q + 1) * LANES]
            turned.append(pltpu.roll(piece, CHUNK * r, 1) if r else piece)
        for k in range(PER):
            store(seat(q * PER + k), pick(groups, [turned[(l - k) % PER] for l in range(PER)]))


def collect(ref, group):
    chunks, rows, _ = ref.shape
    lanes = slice(group * LANES, (group + 1) * LANES)
    groups = lane_groups(rows)
    columns = []
    for q in range(chunks // PER):
        loaded = [ref[seat(q * PER + k), :, lanes].astype(f32) for k in range(PER)]
        parts = []
        for r in range(PER):
            mixed = pick(groups, [loaded[(l - r) % PER] for l in range(PER)])
            parts.append(pltpu.roll(mixed, LANES - CHUNK * r, 1) if r else mixed)
        columns.append(jnp.concatenate(parts, axis=0))
    return jnp.concatenate(columns, axis=1)


def places():
    return tuple(lax.axis_index(axis) for axis in ALL)


def first_bucket(lens_ref):
    _, _, z, c = places()
    return (z * 2 + c) * (lens_ref.shape[0] // 8)


def row_keep(lens_ref, buckets, rows):
    x, y, _, _ = places()
    spot = (x * 4 + y) * rows + lax.broadcasted_iota(jnp.int32, (rows, 1), 0)
    first = first_bucket(lens_ref) + pl.program_id(0) * buckets
    parts = [(spot < lens_ref[first + r]).astype(f32) for r in range(buckets)]
    return jnp.concatenate(parts, axis=0)


def gain_row(gain_ref):
    return gain_ref[...].astype(f32).reshape(1, gain_ref.shape[0])


def rms(values):
    scale = lax.rsqrt(jnp.mean(values * values, axis=-1, keepdims=True) + EPS)
    return values * scale, scale


def values_kernel(lens_ref, tok_ref, gain_ref, vw_ref, out_ref):
    per, rows, width = tok_ref.shape
    tok = tok_ref[...].reshape(per * rows, width).astype(f32)
    normed, _ = rms(tok)
    hidden = (normed * gain_row(gain_ref)).astype(bf16)
    val = nn(hidden, vw_ref[...]) * row_keep(lens_ref, per, rows)

    size = PER * rows
    for g in range(per // PER):

        def store(chunk, block, g=g):
            out_ref[chunk, :, g * LANES : (g + 1) * LANES] = block.astype(bf16)

        spread(val[g * size : (g + 1) * size], store)


def lane_lengths(lens_ref, lanes):
    x, _, _, _ = places()
    group = lanes // CHUNK
    first = first_bucket(lens_ref)
    lane = lax.broadcasted_iota(jnp.int32, (1, lanes), 1) // CHUNK
    lens = jnp.zeros((1, lanes), jnp.int32)
    for n in range(group):
        m, l = divmod(n, PER)
        lens = jnp.where(lane == n, lens_ref[first + m * PER + (l - x + PER) % PER], lens)
    return lens


def mix_kernel(lens_ref, *refs):
    count = len(refs) - 12
    pieces = refs[:count]
    held_ref, exp_out, inv_out, mix_out = refs[count : count + 4]
    landed, held, keep, expo, inverse, mixed, sems, out_sems = refs[count + 4 :]
    span, lanes = held.shape
    x, _, z, c = places()
    half = pieces[0].shape[0] // 2
    copies = [
        pltpu.make_async_copy(piece, landed.at[n], sems.at[n]) for n, piece in enumerate(pieces)
    ]
    held_copy = pltpu.make_async_copy(held_ref, held, sems.at[count])
    copies[0].start()
    held_copy.start()
    for copy in copies[1:]:
        copy.start()
    lens = lane_lengths(lens_ref, lanes)
    place = lax.broadcasted_iota(jnp.int32, (span, lanes), 0)
    keep[...] = (place < lens).astype(f32).astype(bf16)
    out_copies = []
    deep = 4 * 2 * half
    for batch in range(2):
        starts = []
        bounds = []
        for n in range(4 * batch, 4 * batch + 4):
            copies[n].wait()
            core = c if batch == 0 else 1 - c
            ring = (z - n % 4 + 4) % 4
            for k in range(2):
                start = ((core * 2 + (x + k) % 2) * 4 + ring) * half
                starts.append(pl.multiple_of(start, half))
                bounds.append(lens - start)
        cut = pl.ds(4 * batch, 4)
        logits = landed[cut].reshape(deep, span).astype(f32)
        part = jnp.exp(logits - jnp.max(logits, axis=-1, keepdims=True)).astype(bf16)
        expo[cut] = part.reshape(4, 2 * half, span)
        totals = nn(part, keep[...])
        row = lax.broadcasted_iota(jnp.int32, (half, lanes), 0)
        kept = jnp.concatenate([(row < bound).astype(f32) for bound in bounds], axis=0)
        inverted = kept / totals
        inverse[cut] = inverted.reshape(4, 2 * half, lanes)
        if batch == 0:
            held_copy.wait()
        mixed[cut] = (nn(part, held[...]) * inverted).astype(bf16).reshape(4, 2 * half, lanes)
        for n in range(4 * batch, 4 * batch + 4):
            for j, (source, target) in enumerate(
                ((mixed, mix_out), (expo, exp_out), (inverse, inv_out))
            ):
                for k in range(2):
                    copy = pltpu.make_async_copy(
                        source.at[n, pl.ds(k * half, half), :],
                        target.at[pl.ds(starts[2 * (n - 4 * batch) + k], half), :],
                        out_sems.at[n, j, k],
                    )
                    copy.start()
                    out_copies.append(copy)
    for copy in out_copies:
        copy.wait()


def unmix_kernel(exp_ref, gm_ref, inv_ref, mixed_ref, out_ref, g_ref, r_ref):
    @pl.when(pl.program_id(0) == 0)
    def _():
        scaled = gm_ref[...].astype(f32) * inv_ref[...]
        g_ref[...] = scaled.astype(bf16)
        r_ref[...] = (scaled * mixed_ref[...].astype(f32)).astype(bf16)

    out_ref[...] = tn(exp_ref[...], g_ref[...]).astype(bf16)


def scores_kernel(lens_ref, g_ref, r_ref, val_ref, own_ref, other_ref, keep_ref):
    span, lanes = val_ref.shape

    @pl.when(pl.program_id(0) == 0)
    def _():
        place = lax.broadcasted_iota(jnp.int32, (span, lanes), 0)
        keep_ref[...] = (place < lane_lengths(lens_ref, lanes)).astype(f32).astype(bf16)

    out = (nt(g_ref[...], val_ref[...]) - nt(r_ref[...], keep_ref[...])).astype(bf16)
    step = pl.program_id(0)
    _, _, _, c = places()
    rings, bits, rows, _ = own_ref.shape

    def store(ref):
        for bit in range(bits):
            for n in range(rings):
                first = (bit * rings + n) * rows
                ref[n, bit] = out[first : first + rows]

    @pl.when(step == c)
    def _():
        store(own_ref)

    @pl.when(step != c)
    def _():
        store(other_ref)


def ffn_kernel(lens_ref, *refs):
    ins, refs = refs[:7], refs[7:]
    tok_in, cot_in, mix_in, ow_in, gain_ref, up_in, down_in = ins
    out_ref, gr_ref, gm_ref, own_ref, other_ref = refs[:5]
    tok_v, cot_v, mix_v, ow_v, up_v, down_v, out_v, gr_v, gm_v, own_v, other_v, grad_v = refs[5:17]
    sems, out_sems = refs[17:]
    per, rows, width = tok_v.shape
    n = per * rows
    ff = up_v.shape[1]
    step = width
    _, _, _, core = places()
    half = width // 2
    deep = own_v.shape[1] - 2 * width

    def fetch(k, source, target):
        copy = pltpu.make_async_copy(source, target, sems.at[k])
        copy.start()
        return copy

    mix_copy = fetch(0, mix_in, mix_v)
    ow_copy = fetch(1, ow_in, ow_v)
    tok_copy = fetch(2, tok_in, tok_v)
    up_copy = fetch(3, up_in, up_v)
    cot_copy = fetch(4, cot_in, cot_v)
    down_copy = fetch(5, down_in, down_v)
    sent = []

    def send(source, target):
        copy = pltpu.make_async_copy(source, target, out_sems.at[len(sent)])
        copy.start()
        sent.append(copy)

    keep = row_keep(lens_ref, per, rows)
    mix_copy.wait()
    mixed = jnp.concatenate([collect(mix_v, g) for g in range(per // PER)], axis=0).astype(bf16)
    ow_copy.wait()
    tok_copy.wait()
    resid = tok_v[...].reshape(n, width).astype(f32) + nn(mixed, ow_v[...])
    normed, scale = rms(resid)
    gain = gain_row(gain_ref)
    hidden = (normed * gain).astype(bf16)
    cot_copy.wait()
    grad_low = (cot_v[...].reshape(n, width).astype(f32) * keep).astype(bf16)
    up_copy.wait()

    def add(ref, spot, side, source):
        lanes = pl.ds(pl.multiple_of(side * half, half), half)
        ref[spot] = grad_v[source, lanes].astype(bf16)

    def split(spot, source):
        add(other_v, spot, 1 - core, source)
        add(own_v, spot, core, source)

    ffn = jnp.zeros((n, width), f32)
    grad_hidden = jnp.zeros((n, width), f32)
    everything = slice(0, width)
    for q in range(ff // step):
        cut = slice(q * step, (q + 1) * step)
        up = up_v[:, cut]
        pre = nn(hidden, up)
        cdf = 0.5 * (1.0 + lax.erf(pre * ROOT_HALF))
        slope = cdf + pre * jnp.exp(-0.5 * pre * pre) * DENSITY
        act = (pre * cdf).astype(bf16)
        if q == 0:
            down_copy.wait()
        down = down_v[cut, :]
        ffn = ffn + nn(act, down)
        grad_pre = (nt(grad_low, down) * slope).astype(bf16)
        grad_hidden = grad_hidden + nt(grad_pre, up)
        grad_v[...] = tn(act, grad_low)
        split((q, slice(0, width), slice(None)), everything)
        grad_v[...] = tn(hidden, grad_pre)
        split((q, slice(width, 2 * width), slice(None)), everything)
        first = pl.ds(0, 2 * width)
        send(other_v.at[q, first, :], other_ref.at[q, first, :])
        send(own_v.at[q, first, :], own_ref.at[q, first, :])
    weighted = grad_hidden * gain
    back = scale * (weighted - normed * jnp.mean(weighted * normed, axis=-1, keepdims=True))
    grad_resid = grad_low.astype(f32) + back
    gr_v[...] = grad_resid
    send(gr_v, gr_ref)
    grad_att = grad_resid.astype(bf16)
    grad_v[...] = tn(mixed, grad_att)
    for q in range(ff // step):
        split((q, slice(2 * width, 2 * width + deep), slice(None)), slice(q * deep, (q + 1) * deep))
        last = pl.ds(2 * width, deep)
        send(other_v.at[q, last, :], other_ref.at[q, last, :])
        send(own_v.at[q, last, :], own_ref.at[q, last, :])
    out_v[...] = ((resid + ffn) * keep).astype(bf16).reshape(per, rows, width)
    send(out_v, out_ref)
    grad_mixed = nt(grad_att, ow_v[...]) * keep
    size = PER * rows
    for g in range(per // PER):

        def store(chunk, block, g=g):
            gm_v[chunk, :, g * LANES : (g + 1) * LANES] = block.astype(bf16)

        spread(grad_mixed[g * size : (g + 1) * size], store)
    send(gm_v, gm_ref)
    for copy in sent:
        copy.wait()


def value_grad_kernel(lens_ref, tok_ref, vg_ref, gain_ref, ffn_ref, vgrad_ref, joint_ref, acc_ref):
    per, rows, width = tok_ref.shape
    tok = tok_ref[...].reshape(per * rows, width).astype(f32)
    normed, _ = rms(tok)
    hidden = (normed * gain_row(gain_ref)).astype(bf16)
    vgrad = jnp.concatenate([collect(vg_ref, g) for g in range(per // PER)], axis=0)
    vgrad = (vgrad * row_keep(lens_ref, per, rows)).astype(bf16)
    vgrad_ref[...] = vgrad

    @pl.when(pl.program_id(0) == 0)
    def _():
        acc_ref[...] = jnp.zeros_like(acc_ref)

    acc_ref[...] += tn(hidden, vgrad)

    @pl.when(pl.program_id(0) == pl.num_programs(0) - 1)
    def _():
        count, tall, half = joint_ref.shape
        deep = ffn_ref.shape[1]
        rows_here = (tall - deep) // 2
        joint_ref[:, :deep, :] = ffn_ref[...]
        for n in range(count):
            for k in range(2):
                joint_ref[n, deep + k * rows_here : deep + (k + 1) * rows_here, :] = acc_ref[
                    n * rows_here : (n + 1) * rows_here, k * half : (k + 1) * half
                ].astype(bf16)


def input_grad_kernel(tok_ref, vgrad_ref, gr_ref, gain_ref, vw_ref, out_ref):
    per, rows, width = tok_ref.shape
    tok = tok_ref[...].reshape(per * rows, width).astype(f32)
    normed, scale = rms(tok)
    weighted = nt(vgrad_ref[...], vw_ref[...]) * gain_row(gain_ref)
    back = scale * (weighted - normed * jnp.mean(weighted * normed, axis=-1, keepdims=True))
    out_ref[...] = (gr_ref[...] + back).reshape(per, rows, width)


def joint_sum_kernel(joint_ref, ffn_ref, value_ref):
    total = jnp.sum(joint_ref[...].astype(f32), axis=0).astype(bf16)
    deep = ffn_ref.shape[1]
    ffn_ref[...] = jnp.broadcast_to(total[None, :deep], ffn_ref.shape)
    value_ref[...] = total[deep:]


def ring_spread_kernel(*refs):
    parts, out_ref, held = refs[:4], refs[4], refs[5]
    me = lax.axis_index("z")
    for k, part in enumerate(parts):
        held[(me - k + 4) % 4] = part[...].astype(f32)
    total = (held[0] + held[1]) + (held[2] + held[3])
    out_ref[...] = jnp.broadcast_to(total[None], out_ref.shape).astype(bf16)


def row_total(product):
    folded = sum(
        product[:, n * LANES : (n + 1) * LANES] for n in range(product.shape[1] // LANES)
    )
    return jnp.sum(folded.T, axis=0, keepdims=True)


def fold_kernel(own_ref, got_ref, *outs):
    _, _, z, _ = places()
    for k, out in enumerate(outs):
        n = (z + k) % 4
        out[...] = (own_ref[n].astype(f32) + got_ref[n].astype(f32)).astype(bf16)


def sum_kernel(*refs):
    parts, out_ref = refs[:-1], refs[-1]
    out_ref[...] = sum(part[...].astype(f32) for part in parts).astype(bf16)


def split_sum_kernel(*refs):
    parts, (own_ref, other_ref) = refs[:4], refs[4:]
    total = sum(part[...].astype(f32) for part in parts).astype(bf16)
    odd = places()[0] % 2 == 1
    own_ref[...] = jnp.where(odd, total[1], total[0])
    other_ref[...] = jnp.where(odd, total[0], total[1])


def logits_grad_kernel(part_ref, logits_ref, out_ref):
    logits = logits_ref[0].astype(f32)
    exact = jnp.exp(logits - jnp.max(logits, axis=-1, keepdims=True))
    out_ref[0] = part_ref[...].astype(f32) * exact


def finish_ffn_kernel(*refs):
    pieces, (up_ref, gain_ref), (down_out, up_out, ow_out, gain_out) = refs[:8], refs[8:10], refs[10:14]
    landed, wide, up, sems, out_sems = refs[14:]
    width = up.shape[0]
    half = landed.shape[2]
    deep = landed.shape[1] - 2 * width
    _, _, z, c = places()
    copies = [
        pltpu.make_async_copy(piece, landed.at[n], sems.at[n]) for n, piece in enumerate(pieces)
    ]
    up_copy = pltpu.make_async_copy(up_ref, up, sems.at[8])
    copies[0].start()
    up_copy.start()
    for copy in copies[1:]:
        copy.start()
    product = jnp.zeros((width, half), f32)
    out_copies = []
    for n, copy in enumerate(copies):
        copy.wait()
        ring = (z - n % 4 + 4) % 4
        side = c if n < 4 else 1 - c
        wide[n] = landed[n].astype(f32)
        lanes = pl.ds(pl.multiple_of(side * half, half), half)
        columns = pl.ds(pl.multiple_of((2 * ring + side) * half, half), half)
        targets = (
            (0, width, down_out.at[pl.ds(pl.multiple_of(ring * width, width), width), lanes]),
            (width, width, up_out.at[:, columns]),
            (2 * width, deep, ow_out.at[pl.ds(pl.multiple_of(ring * deep, deep), deep), lanes]),
        )
        for k, (first, tall, target) in enumerate(targets):
            out_copy = pltpu.make_async_copy(
                wide.at[n, pl.ds(first, tall), :], target, out_sems.at[n, k]
            )
            out_copy.start()
            out_copies.append(out_copy)
        if n == 0:
            up_copy.wait()
        product = product + up[:, columns].astype(f32) * wide[n, width : 2 * width, :]
    gain_out[...] = row_total(product) / gain_row(gain_ref)
    for out_copy in out_copies:
        out_copy.wait()


def finish_value_kernel(in_ref, vw_ref, gain_ref, out_ref, gain_out):
    count, tall, half = in_ref.shape
    rows_here = tall // 2
    for n in range(count):
        for k in range(2):
            out_ref[n * rows_here : (n + 1) * rows_here, k * half : (k + 1) * half] = in_ref[
                n, k * rows_here : (k + 1) * rows_here
            ].astype(f32)
    gain_out[...] = row_total(vw_ref[...].astype(f32) * out_ref[...]) / gain_row(gain_ref)


def params(mib):
    return pltpu.CompilerParams(vmem_limit_bytes=mib * 1024 * 1024)


def cost(flops, size):
    return pl.CostEstimate(flops=int(flops), bytes_accessed=int(size), transcendentals=0)


def whole(*shape):
    return pl.BlockSpec(shape, lambda *_: (0,) * len(shape))


def once(*shape):
    return pl.BlockSpec(shape, lambda *_: (0,) * len(shape), pipeline_mode=pl.Buffered(1))


def shaped(dtype, *shape):
    return pltpu.HBM(shape, dtype)


def stay(*arrays):
    return [pltpu.with_memory_space_constraint(array, pltpu.HBM) for array in arrays]


def flat(x, y, z, c):
    return ((x % 4) * 4 + y % 4) * 8 + (z % 4) * 2 + c % 2


def devices():
    for i in range(128):
        s, h = divmod(i, 8)
        yield i, s // 4, s % 4, h // 2, h % 2


def shift(array, axis, step):
    return lax.ppermute(array, axis, [(i, (i + step) % 4) for i in range(4)])


def flip(array):
    return lax.ppermute(array, "core", [(0, 1), (1, 0)])


def flip_x(array):
    return lax.ppermute(array, "x", [(i, i ^ 1) for i in range(4)])


def to_plane(array, back=False):
    pairs = [(i, flat(2 * e + (a & 1), d, b, a >> 1)) for i, a, b, d, e in devices()]
    if back:
        pairs = [(j, i) for i, j in pairs]
    return lax.ppermute(array, ALL, pairs)


def around(parts, axis):
    return [parts[0]] + [shift(parts[step], axis, step) for step in (1, 2, 3)]


def swap(array, axes):
    return lax.all_to_all(array, axes, 0, 0, tiled=True)


def swap_seq(array):
    return swap(array, PLANE)


def after(array, *others):
    return lax.optimization_barrier((array,) + others)[0]


def ordered(arrays, *others):
    return list(lax.optimization_barrier((*arrays, *others)))[: len(arrays)]


def shards(
    tokens,
    lengths,
    norm_gain,
    value_weight,
    synth_logits,
    out_weight,
    ffn_gain,
    up_weight,
    down_weight,
    cotangent,
):
    group, rows, width = tokens.shape
    span = synth_logits.shape[2]
    ff = up_weight.shape[1]
    blocks = span // rows
    total_rows = group * rows
    steps = group // PER
    tile = PER * rows

    def tok_spec(n):
        return pl.BlockSpec((n, rows, width), lambda m, *_: (m, 0, 0))

    def move_spec(n):
        return pl.BlockSpec((blocks, rows, n // PER * LANES), lambda m, *_: (0, 0, m))

    def row_spec(n, columns):
        return pl.BlockSpec((n, columns), lambda m, *_: (m, 0))

    def call(kernel, grid, ins, outs, shapes, flops, size, scratch=(), prefetch=0, long=False, mib=40):
        return pl.pallas_call(
            kernel,
            grid_spec=pltpu.PrefetchScalarGridSpec(
                num_scalar_prefetch=prefetch,
                grid=grid,
                in_specs=ins,
                out_specs=outs,
                scratch_shapes=scratch,
            ),
            out_shape=shapes,
            compiler_params=params(mib),
            cost_estimate=cost(1e13, 1e6) if long else cost(1e6, 1e5),
        )

    with jax.named_scope("logits"):
        block = synth_logits.reshape(rows, span)
        block = to_plane(block)

    with jax.named_scope("values"):
        sent_values = call(
            values_kernel,
            (1,),
            [tok_spec(group), whole(width), whole(width, width)],
            move_spec(group),
            shaped(bf16, blocks, rows, width),
            2 * total_rows * width * width,
            3e6,
            prefetch=1,
        )(lengths, *stay(tokens, norm_gain, value_weight))
        block = ordered([block], sent_values)[0]

    with jax.named_scope("logits"):
        other = flip_x(block)
        pair = jnp.concatenate([block, other])
        held = swap_seq(ordered([sent_values], other)[0]).reshape(span, width)
        pieces = [pair] + [shift(pair, "z", step) for step in (1, 2, 3)]
        pieces = pieces + [flip(piece) for piece in pieces]

    quarter = span // 4
    anywhere = pl.BlockSpec(memory_space=pl.ANY)
    with jax.named_scope("mix"):
        expo, inverse, mixed_held = call(
            mix_kernel,
            (1,),
            [anywhere] * 9,
            [anywhere] * 3,
            [shaped(bf16, span, span), shaped(f32, span, width), shaped(bf16, span, width)],
            4 * span * span * width,
            8e6,
            scratch=[
                pltpu.VMEM((8, 2 * rows, span), bf16),
                pltpu.VMEM((span, width), bf16),
                pltpu.VMEM((span, width), bf16),
                pltpu.VMEM((8, 2 * rows, span), bf16),
                pltpu.VMEM((8, 2 * rows, width), f32),
                pltpu.VMEM((8, 2 * rows, width), bf16),
                pltpu.SemaphoreType.DMA((9,)),
                pltpu.SemaphoreType.DMA((8, 3, 2)),
            ],
            prefetch=1,
        )(lengths, *pieces, held)
        got_mixed = swap_seq(mixed_held.reshape(blocks, rows, width))

    tall = ff // 4 + width + width // 4
    half_width = width // 2
    grads_shape = (4, tall, half_width)
    with jax.named_scope("ffn"):
        output, grad_resid, sent_grad, own_part, other_part = call(
            ffn_kernel,
            (1,),
            [anywhere] * 4 + [whole(width)] + [anywhere] * 2,
            [anywhere] * 5,
            [
                shaped(bf16, group, rows, width),
                shaped(f32, total_rows, width),
                shaped(bf16, blocks, rows, width),
                shaped(bf16, *grads_shape),
                shaped(bf16, *grads_shape),
            ],
            2 * total_rows * width * (6 * ff + 3 * width),
            2e7,
            scratch=[
                pltpu.VMEM((group, rows, width), bf16),
                pltpu.VMEM((group, rows, width), bf16),
                pltpu.VMEM((blocks, rows, width), bf16),
                pltpu.VMEM((width, width), bf16),
                pltpu.VMEM((width, ff), bf16),
                pltpu.VMEM((ff, width), bf16),
                pltpu.VMEM((group, rows, width), bf16),
                pltpu.VMEM((total_rows, width), f32),
                pltpu.VMEM((blocks, rows, width), bf16),
                pltpu.VMEM(grads_shape, bf16),
                pltpu.VMEM(grads_shape, bf16),
                pltpu.VMEM((width, width), f32),
                pltpu.SemaphoreType.DMA((6,)),
                pltpu.SemaphoreType.DMA((4 * ff // width + 3,)),
            ],
            prefetch=1,
            mib=54,
        )(
            lengths,
            *stay(tokens, cotangent), got_mixed, *stay(out_weight, ffn_gain, up_weight, down_weight),
        )
        got_grad = swap_seq(sent_grad).reshape(span, width)

    def fold(own, got):
        shape = own.shape[1:]
        return call(
            fold_kernel,
            (1,),
            [whole(4, *shape)] * 2,
            [whole(*shape)] * 4,
            [shaped(bf16, *shape)] * 4,
            1e6,
            6 * math.prod(own.shape),
        )(*stay(own), got)

    with jax.named_scope("ffn_sum"):
        folded = fold(own_part, flip(other_part))
        ring_parts = around(folded, "z")
        got_grad = ordered([got_grad], folded[0])[0]

    with jax.named_scope("unmix"):
        held_grad, g_scaled, r_scaled = call(
            unmix_kernel,
            (2,),
            [pl.BlockSpec((span, 2 * quarter), lambda j: (0, j))] + [once(span, width)] * 3,
            [row_spec(2 * quarter, width), whole(span, width), whole(span, width)],
            [shaped(bf16, span, width)] * 3,
            2 * span * span * width,
            9e6,
        )(*stay(expo), got_grad, *stay(inverse, mixed_held))
        got_values = swap_seq(held_grad.reshape(blocks, rows, width))


    with jax.named_scope("scores"):
        score_shape = (4, 2, rows, span)
        own_scores, other_scores = call(
            scores_kernel,
            (2,),
            [row_spec(2 * quarter, width), row_spec(2 * quarter, width), whole(span, width)],
            [whole(*score_shape)] * 2,
            [shaped(bf16, *score_shape)] * 2,
            4 * span * span * width,
            8e6,
            scratch=[pltpu.VMEM((span, width), bf16)],
            prefetch=1,
        )(lengths, *stay(g_scaled, r_scaled), ordered([held], held_grad)[0])
        got_scores = flip(other_scores)

    with jax.named_scope("ffn_sum"):
        part = row_spec(tall // 2, half_width)
        ring_parts = ordered(ring_parts, own_scores)
        ffn_sum = call(
            sum_kernel,
            (2,),
            [part] * 4,
            part,
            shaped(bf16, tall, half_width),
            1e6,
            3e6,
            long=True,
        )(*ring_parts)

    with jax.named_scope("score_sum"):
        score_parts = fold(*ordered([own_scores, got_scores], ffn_sum))
        score_ring = around(score_parts, "z")
        got_values = ordered([got_values], score_parts[0])[0]

    with jax.named_scope("ffn_sum"):
        piece = tall // blocks
        ffn_sum = ffn_sum.reshape(blocks, piece, half_width)
        joint = piece + 2 * (width // blocks)

    with jax.named_scope("value_grad"):
        value_grad, joint_part = call(
            value_grad_kernel,
            (1,),
            [tok_spec(group), move_spec(group), whole(width), whole(blocks, piece, half_width)],
            [row_spec(total_rows, width), whole(blocks, joint, half_width)],
            [shaped(bf16, total_rows, width), shaped(bf16, blocks, joint, half_width)],
            2 * total_rows * width * width,
            4e6,
            scratch=[pltpu.VMEM((width, width), f32)],
            prefetch=1,
        )(lengths, *stay(tokens), got_values, *stay(norm_gain), ffn_sum)
        got_joint = swap_seq(joint_part)

    with jax.named_scope("score_sum"):
        own_scores, other_scores = call(
            split_sum_kernel,
            (1,),
            [whole(2, rows, span)] * 4,
            [whole(rows, span)] * 2,
            [shaped(bf16, rows, span)] * 2,
            1e6,
            2e6,
            long=True,
        )(*ordered(score_ring, joint_part))
        got_scores = flip_x(other_scores)

    with jax.named_scope("input_grad"):
        input_grad = call(
            input_grad_kernel,
            (steps // 2,),
            [
                tok_spec(2 * PER),
                row_spec(2 * tile, width),
                row_spec(2 * tile, width),
                whole(width),
                whole(width, width),
            ],
            tok_spec(2 * PER),
            shaped(f32, group, rows, width),
            2 * total_rows * width * width,
            7e6,
        )(*stay(tokens), value_grad, *stay(*ordered([grad_resid], own_scores), norm_gain, value_weight))

    with jax.named_scope("score_sum"):
        score_total = call(
            sum_kernel,
            (1,),
            [whole(rows, span)] * 2,
            whole(rows, span),
            shaped(bf16, rows, span),
            1e6,
            1e6,
        )(*ordered([own_scores, got_scores], input_grad))
        score_back = to_plane(score_total, back=True)

    with jax.named_scope("joint_sum"):
        few = (joint - piece, half_width)
        ffn_spread, small = call(
            joint_sum_kernel,
            (1,),
            [whole(blocks, joint, half_width)],
            [whole(blocks, piece, half_width), whole(*few)],
            [shaped(bf16, blocks, piece, half_width), shaped(bf16, *few)],
            1e6,
            2e6,
        )(*ordered([got_joint], score_total))

    with jax.named_scope("value_sum"):
        small = call(
            sum_kernel,
            (1,),
            [whole(*few)] * 2,
            whole(*few),
            shaped(bf16, *few),
            1e6,
            1e6,
        )(small, flip(small))
        value_spread = call(
            ring_spread_kernel,
            (1,),
            [whole(*few)] * 4,
            whole(blocks, *few),
            shaped(bf16, blocks, *few),
            1e6,
            1e6,
            scratch=[pltpu.VMEM((4, *few), f32)],
        )(*around([small] * 4, "z"))

    with jax.named_scope("score_sum"):
        logits_grad = call(
            logits_grad_kernel,
            (1,),
            [whole(rows, span), whole(1, rows, span)],
            whole(1, rows, span),
            shaped(f32, 1, rows, span),
            1e6,
            1e6,
        )(*ordered([score_back], value_spread), synth_logits)

    with jax.named_scope("ffn_sum"):
        ffn_sum = ordered([swap_seq(ffn_spread)], value_spread)[0].reshape(tall, half_width)
        pieces = around([ffn_sum] * 4, "z")

    with jax.named_scope("value_sum"):
        value_sum = swap_seq(ordered([value_spread], ffn_sum)[0])

    with jax.named_scope("value_sum"):
        value_weight_grad, norm_gain_grad = call(
            finish_value_kernel,
            (1,),
            [whole(blocks, *few), whole(width, width), whole(width)],
            [whole(width, width), whole(1, width)],
            [shaped(f32, width, width), shaped(f32, 1, width)],
            4e6,
            2e6,
        )(value_sum, *stay(value_weight, norm_gain))

    with jax.named_scope("ffn_sum"):
        pieces = ordered(pieces, value_weight_grad, logits_grad)
        pieces = pieces + [flip(part) for part in pieces]
        down_grad, up_grad, out_grad, ffn_gain_grad = call(
            finish_ffn_kernel,
            (1,),
            [anywhere] * 9 + [whole(width)],
            [anywhere] * 3 + [whole(1, width)],
            [
                shaped(f32, ff, width),
                shaped(f32, width, ff),
                shaped(f32, width, width),
                shaped(f32, 1, width),
            ],
            4e6,
            13e6,
            scratch=[
                pltpu.VMEM((8, tall, half_width), bf16),
                pltpu.VMEM((8, tall, half_width), f32),
                pltpu.VMEM((width, ff), bf16),
                pltpu.SemaphoreType.DMA((9,)),
                pltpu.SemaphoreType.DMA((8, 3)),
            ],
        )(*pieces, *stay(up_weight, ffn_gain))

    return (
        output,
        input_grad,
        norm_gain_grad.reshape(width),
        value_weight_grad,
        logits_grad,
        out_grad,
        ffn_gain_grad.reshape(width),
        up_grad,
        down_grad,
    )


def solution(mesh):
    token_spec = P(("z", "core"), PLANE, None)
    placed = (
        token_spec,
        P(),
        P(),
        P(),
        token_spec,
        P(),
        P(),
        P(),
        P(),
        token_spec,
    )
    fine = jax.sharding.Mesh(mesh.devices.reshape(4, 4, 4, 2), ALL)
    return jax.shard_map(
        shards,
        mesh=fine,
        in_specs=placed,
        out_specs=(token_spec, token_spec, P(), P(), token_spec, P(), P(), P(), P()),
        check_vma=False,
    )
```
